32 devices in a mesh: group: 4 (over z), seq: 4 (over y, core), dp: 2 (over x).
Axes of the slice: x: 2, y: 2, z: 4, core: 2. Of those that a mesh axis runs over, the one named last changes fastest.
Arguments:
- noise_gen: bfloat16 [4, 1024, 64], P('dp', 'seq'), may hold values from -6 to 6
- noise_score: bfloat16 [4, 1024, 64], P('dp', 'seq'), may hold values from -6 to 6
- prev_latents: float32 [4, 1024, 64], P('dp', 'seq'), may hold values from -42 to 42
- t_idx: int32 [4], P('dp'), may hold values from 0 to 999
- w_in: bfloat16 [4, 64, 3072], P('group'), may hold values from -4 to 4, as said below
- w_qkv: bfloat16 [4, 3072, 3, 512], P('group', None, None, 'seq'), may hold values from -4 to 4, as said below
- w_out: bfloat16 [4, 512, 64], P('group', 'seq'), may hold values from -4 to 4, as said below
- w_final: bfloat16 [4, 3072, 64], P('group'), may hold values from -4 to 4, as said below
- mod_scale: float32 [4, 3072], P('group'), may hold values from -0.5 to 0.5
- mod_shift: float32 [4, 3072], P('group'), may hold values from -3 to 3
- saved_features: bfloat16 [4, 1024, 3072], P('dp', 'seq'), may hold values from -6 to 6
Outputs:
- predictions: float32 [4, 4, 1024, 64], P('group', 'dp', 'seq')
- dmd_grad: float32 [4, 1024, 64], P('dp', 'seq')
- gen_final_grad: float32 [3072, 64], replicated
The draws below stay inside these ranges and needn't reach their ends.
Inputs may be any that keep to these rules, and one draw needn't show every extreme that they name: `w_in`: groups 1 and 2 hold equal weights. `w_qkv`: groups 1 and 2 hold equal weights. `w_out`: groups 1 and 2 hold equal weights. `w_final`: groups 1 and 2 hold equal weights.
All inputs are finite; a program needn't handle non-finite values. Where the reference program divides by a largest or mean magnitude, that divisor is 1e-20 or more.
Results may differ from the reference program's by a relative error of at most 0.017.
Values may be sent and summed in bfloat16 or wider, within the bound.
A program may use at most 128 MiB of HBM per device.

```python
import math
import jax
import jax.numpy as jnp
from jax import lax

D = 3072
HD = 128
PATCH = 64
NTOK = 1024
NOISE_LEVEL_COUNT = 1000
HEADS = 4
IMAGES = 4


def grouped(key, shape, fan):
    base = jnp.clip(jax.random.normal(key, (3,) + shape, jnp.float32), -4.0, 4.0) * fan ** (-0.5)
    return jnp.stack([base[0], base[1], base[1], base[2]]).astype(jnp.bfloat16)


def draw_w_in(key, part):
    key = jax.random.fold_in(key, 21)
    return grouped(key, (PATCH, D), PATCH)


def draw_w_qkv(key, part):
    key = jax.random.fold_in(key, 22)
    return grouped(key, (D, 3, HEADS * HD), D)


def draw_w_out(key, part):
    key = jax.random.fold_in(key, 23)
    return grouped(key, (HEADS * HD, PATCH), HEADS * HD)


def draw_w_final(key, part):
    key = jax.random.fold_in(key, 24)
    return grouped(key, (D, PATCH), D)


def draw_prev_latents(key, part):
    key = jax.random.fold_in(key, 25)
    first, second_operand = jax.random.split(key)
    token_position = jnp.arange(NTOK, dtype=jnp.float32) / NTOK
    rough = jnp.exp(jax.random.uniform(second_operand, (IMAGES, NTOK, 1), jnp.float32, 0.0, math.log(3.5)))
    factor = 3.0 ** token_position[None, :, None] * rough
    base = jnp.clip(jax.random.normal(first, (IMAGES, NTOK, PATCH), jnp.float32), -4.0, 4.0)
    return base * factor


def touch_ends(values, key, smallest, largest):
    index_at = [jax.random.randint(jax.random.fold_in(key, axis), (), 0, length) for axis, length in enumerate(values.shape)]
    longest = values.shape.index(max(values.shape))
    neighbour = index_at[:longest] + [(index_at[longest] + 1) % values.shape[longest]] + index_at[longest + 1:]
    return values.at[tuple(index_at)].set(smallest).at[tuple(neighbour)].set(largest)


def block_scale(stream_key, dims, pieces, least, largest):
    loudness = 1.0
    for axis_at, shards_of in pieces:
        heights = jax.random.uniform(jax.random.fold_in(jax.random.fold_in(stream_key, 6), axis_at), (shards_of,), jnp.float32, least / len(pieces), largest / len(pieces))
        loudness = loudness * jnp.repeat(jnp.exp(heights), dims[axis_at] // shards_of).reshape((-1,) + (1,) * (len(dims) - 1 - axis_at))
    return loudness


def noise(key, shape, deviation, limit, cuts=(), kind=jnp.bfloat16):
    array = jax.random.normal(key, shape, jnp.float32) * deviation
    if len(cuts) > 0:
        array = block_scale(key, shape, cuts, -0.22, 0.18) * array
    return jnp.clip(array, min=-limit, max=limit).astype(kind)


def setup_inputs(seed: int = 0) -> dict:
    splits = jax.random.split(jax.random.key(seed), 12)
    noise_gen = noise(splits[0], (IMAGES, NTOK, PATCH), 1.0, 6.0, ((0, 2), (1, 4)))
    noise_score = noise(splits[1], (IMAGES, NTOK, PATCH), 1.0, 6.0, ((0, 2), (1, 4)))
    prev_latents = draw_prev_latents(jax.random.fold_in(splits[11], 71), 0)
    t_idx = touch_ends(jax.random.randint(splits[3], (IMAGES,), 0, NOISE_LEVEL_COUNT), jax.random.fold_in(splits[3], 1), 0, NOISE_LEVEL_COUNT - 1).astype(jnp.int32)
    w_in = draw_w_in(jax.random.fold_in(splits[11], 71), 0)
    w_qkv = draw_w_qkv(jax.random.fold_in(splits[11], 71), 0)
    w_out = draw_w_out(jax.random.fold_in(splits[11], 71), 0)
    w_final = draw_w_final(jax.random.fold_in(splits[11], 71), 0)
    mod_scale = jnp.clip(jax.random.uniform(splits[8], (4, D), jnp.float32, -0.5, 0.5) * block_scale(splits[8], (4, D), ((0, 4),), -0.4, 0.0), -0.5, 0.5)
    mod_shift = noise(splits[9], (4, D), 0.5, 3.0, ((0, 4),), jnp.float32)
    saved_features = noise(splits[10], (IMAGES, NTOK, D), 1.0, 6.0, ((0, 2), (1, 4)))
    return {"noise_gen": noise_gen, "noise_score": noise_score, "prev_latents": prev_latents, "t_idx": t_idx, "w_in": w_in, "w_qkv": w_qkv, "w_out": w_out, "w_final": w_final, "mod_scale": mod_scale, "mod_shift": mod_shift, "saved_features": saved_features}


def rounded(value_rows):
    return lax.optimization_barrier(value_rows.astype(jnp.bfloat16)).astype(jnp.float32)

def model_pass(model_input, noise_level, w_in, w_qkv, w_out, w_final, scale, shift):
    projected = jnp.einsum('inp,pd->ind', model_input.astype(jnp.bfloat16).astype(jnp.float32), w_in.astype(jnp.float32))
    normed = projected * lax.rsqrt(lax.optimization_barrier(jnp.mean(projected * projected, axis=-1, keepdims=True)) + 1e-06)
    features = rounded(normed * (1.0 + noise_level[:, None, None] * scale) + shift)
    head_weights = w_qkv.reshape(D, 3, HEADS, HD).transpose(2, 0, 1, 3)
    head_maps = w_out.reshape(HEADS, HD, PATCH)

    def one_head(pair):
        weight, output_layout = pair
        triple = rounded(jnp.einsum('ind,dce->cine', features, weight.astype(jnp.float32)))
        scores = jnp.einsum('iqe,ike->iqk', triple[0], triple[1]) / math.sqrt(HD)
        probs = rounded(jax.nn.softmax(scores, axis=-1))
        attention_result = rounded(jnp.einsum('iqk,ike->iqe', probs, triple[2]))
        return jnp.einsum('iqe,ep->iqp', attention_result, output_layout.astype(jnp.float32))
    terms = lax.map(one_head, (head_weights, head_maps))
    local = jnp.einsum('ind,dp->inp', features, w_final.astype(jnp.float32))
    return local + lax.optimization_barrier(jnp.sum(terms, axis=0))

def reference(noise_gen, noise_score, prev_latents, t_idx, w_in, w_qkv, w_out, w_final, mod_scale, mod_shift, saved_features):
    level = (t_idx.astype(jnp.float32) + 0.5) / NOISE_LEVEL_COUNT
    noisy = (1.0 - level)[:, None, None] * prev_latents + level[:, None, None] * noise_score.astype(jnp.float32)
    outputs = []
    for index in range(4):
        if index == 0:
            model_input = noise_gen.astype(jnp.float32)
            noise_level = jnp.ones_like(level)
        else:
            model_input = noisy
            noise_level = level
        velocity = model_pass(model_input, noise_level, w_in[index], w_qkv[index], w_out[index], w_final[index], mod_scale[index], mod_shift[index])
        outputs.append(model_input - noise_level[:, None, None] * velocity)
    real = outputs[2] + 2.5 * (outputs[1] - outputs[2])
    fake = outputs[3]
    spread = lax.optimization_barrier(jnp.mean(jnp.abs(prev_latents - real), axis=(1, 2))) + 1e-05
    dmd_grad = (fake - real) / spread[:, None, None]
    down = (-dmd_grad).astype(jnp.bfloat16).astype(jnp.float32)
    total = jnp.einsum('ind,inp->dp', saved_features.astype(jnp.float32), down)
    gen_final_grad = total / math.sqrt(IMAGES * NTOK)
    return (jnp.stack(outputs), dmd_grad, gen_final_grad)
```

```python
import functools
import math

import jax
import jax.numpy as jnp
from jax import lax
from jax.experimental import pallas as pl
from jax.experimental.pallas import tpu as pltpu
from jax.sharding import PartitionSpec as P

NTOK = 1024
NOISE_LEVEL_COUNT = 1000


def embed(latent, noise_level, w_in_here, scale, shift):
    projected = jnp.einsum("inp,pd->ind", latent, w_in_here, preferred_element_type=jnp.float32)
    normed = projected * lax.rsqrt(jnp.mean(projected * projected, axis=-1, keepdims=True) + 1e-06)
    return (normed * (1.0 + noise_level[:, None, None] * scale) + shift).astype(jnp.bfloat16)


def per_device_plain(
    noise_gen,
    noise_score,
    prev_latents,
    t_idx,
    w_in,
    w_qkv,
    w_out,
    w_final,
    mod_scale,
    mod_shift,
    saved_features,
):
    model_index = lax.axis_index("group")
    local_image_batch, rows_image, channels = noise_gen.shape
    width = w_in.shape[2]
    head_size = w_out.shape[1]
    level = (t_idx.astype(jnp.float32) + 0.5) / NOISE_LEVEL_COUNT
    noisy = (1.0 - level)[:, None, None] * prev_latents + level[:, None, None] * noise_score.astype(
        jnp.float32
    )
    is_generator = model_index == 0
    model_input = jnp.where(is_generator, noise_gen.astype(jnp.float32), noisy)
    noise_level = jnp.where(is_generator, jnp.ones_like(level), level)
    latent = model_input.astype(jnp.bfloat16)
    w_in_here = w_in[0]
    head_weight = w_qkv[0].reshape(width, 3 * head_size)
    scale = mod_scale[0]
    shift = mod_shift[0]
    features = embed(latent, noise_level, w_in_here, scale, shift)
    triple = jnp.einsum(
        "ind,de->ine",
        lax.all_gather(features, "seq", axis=1, tiled=True),
        head_weight,
        preferred_element_type=jnp.float32,
    ).astype(jnp.bfloat16)
    queries = triple[:, :, :head_size]
    keys = triple[:, :, head_size : 2 * head_size]
    value_rows = triple[:, :, 2 * head_size :]
    scores = jnp.einsum(
        "iqe,ike->iqk", queries, keys, preferred_element_type=jnp.float32
    ) / math.sqrt(head_size)
    probs = jax.nn.softmax(scores, axis=-1).astype(jnp.bfloat16)
    attention_result = jnp.einsum(
        "iqk,ike->iqe", probs, value_rows, preferred_element_type=jnp.float32
    ).astype(jnp.bfloat16)
    token_leading_layout = attention_result.transpose(1, 0, 2)
    output_layout = w_out[0]
    summed = (
        lax.psum_scatter(
            jnp.einsum(
                "sca,af->scf",
                token_leading_layout,
                output_layout,
                preferred_element_type=jnp.float32,
            ).astype(jnp.bfloat16),
            "seq",
            scatter_dimension=0,
            tiled=True,
        )
        .astype(jnp.float32)
        .transpose(1, 0, 2)
    )
    velocity = (
        jnp.einsum("ind,dp->inp", features, w_final[0], preferred_element_type=jnp.float32) + summed
    )
    prediction = model_input - noise_level[:, None, None] * velocity
    real_weight = jnp.where(model_index == 1, 2.5, jnp.where(model_index == 2, -1.5, 0.0))
    fake_weight = jnp.where(model_index == 3, 1.0, 0.0)
    real, fake = lax.psum((real_weight * prediction, fake_weight * prediction), "group")
    deviation = jnp.sum(jnp.abs(prev_latents - real), axis=(1, 2))
    total_dev = lax.psum(deviation, "seq")
    spread = total_dev / (NTOK * channels) + 1e-05
    dmd_grad = (fake - real) / spread[:, None, None]
    down = (-dmd_grad).astype(jnp.bfloat16)
    normalizer = 1.0 / math.sqrt(local_image_batch * lax.axis_size("dp") * NTOK)
    partial_grad = jnp.einsum(
        "ind,inp->dp", saved_features, down, preferred_element_type=jnp.float32
    )
    total_grad = lax.psum(partial_grad, ("seq", "dp"))
    return (prediction[None], dmd_grad, total_grad * normalizer)


F32 = jnp.float32
BF16 = jnp.bfloat16
MESH = pl.DeviceIdType.MESH
PARTS = 3
ROWS = 16


def dot(a, b):
    return jnp.dot(a, b, preferred_element_type=F32)


def dot_first(a, b):
    return lax.dot_general(a, b, (((0,), (0,)), ((), ())), preferred_element_type=F32)


def dot_last(a, b):
    return lax.dot_general(a, b, (((1,), (1,)), ((), ())), preferred_element_type=F32)


def split_parts(x):
    terms = []
    for _ in range(PARTS):
        term = x.astype(BF16)
        terms.append(term)
        x = x - term.astype(F32)
    return terms


def kernel(
    dims,
    t_ref,
    noise_gen_ref,
    noise_score_ref,
    prev_ref,
    w_in_ref,
    w_qkv_hbm,
    w_out_ref,
    w_final_hbm,
    scale_ref,
    shift_ref,
    saved_hbm,
    pred_ref,
    dmd_ref,
    grad_ref,
    w_qkv,
    w_final,
    saved,
    left,
    xg,
    rg,
    noisy,
    keys,
    queries,
    values,
    vel_out,
    vel_in,
    split_out,
    split_in,
    diff,
    dev,
    grad_out,
    grad_in,
    gathered,
    load_sem,
    x_send,
    x_recv,
    r_send,
    r_recv,
    vel_send,
    vel_recv,
    split_send,
    split_recv,
    diff_send,
    diff_recv,
    dev_send,
    dev_recv,
    grad_send,
    grad_recv,
    up_send,
    up_recv,
    all_send,
    all_recv,
):
    n_group, n_seq, n_dp = dims
    n_plane = n_seq * n_dp
    images, channels, toks = prev_ref.shape
    width = w_in_ref.shape[1]
    head = w_out_ref.shape[1]
    share = saved.shape[2]
    chunk = grad_in.shape[2]
    lane_blocks = share // chunk
    g = lax.axis_index("group")
    s = lax.axis_index("seq")
    d = lax.axis_index("dp")
    here = g * n_seq + s
    place = s * n_dp + d

    loads = [
        pltpu.make_async_copy(w_qkv_hbm, w_qkv, load_sem.at[0]),
        pltpu.make_async_copy(w_final_hbm, w_final, load_sem.at[1]),
        pltpu.make_async_copy(
            saved_hbm.at[:, :, pl.ds(pl.multiple_of(g * share, 128), share)], saved, load_sem.at[2]
        ),
    ]
    for load in loads:
        load.start()

    barrier = pltpu.get_barrier_semaphore()
    peers = 0
    for dg in range(n_group):
        for ds in range(n_seq):
            if dg or ds:
                pl.semaphore_signal(
                    barrier,
                    inc=1,
                    device_id={"group": lax.rem(g + dg, n_group), "seq": lax.rem(s + ds, n_seq)},
                    device_id_type=MESH,
                )
                peers += 1
    for ds in range(n_seq):
        for dd in range(1, n_dp):
            pl.semaphore_signal(
                barrier,
                inc=1,
                device_id={"seq": lax.rem(s + ds, n_seq), "dp": lax.rem(d + dd, n_dp)},
                device_id_type=MESH,
            )
            peers += 1

    generator = jnp.where(g == 0, 1.0, 0.0).astype(F32)

    def level(i, lanes):
        return (jnp.full((1, lanes), t_ref[i].astype(F32), F32) + 0.5) / NOISE_LEVEL_COUNT

    def own_level(i, lanes):
        return generator + (1.0 - generator) * level(i, lanes)

    for i in range(images):
        lv = level(i, toks)
        noisy[i] = (1.0 - lv) * prev_ref[i] + lv * noise_score_ref[i].astype(F32)
        model_input = generator * noise_gen_ref[i].astype(F32) + (1.0 - generator) * noisy[i]
        pred_ref[i] = model_input
        xg[0, i] = model_input.astype(BF16)

    pl.semaphore_wait(barrier, peers)

    sends = []

    def send(src, dst, send_sem, recv_sem, device):
        copy = pltpu.make_async_remote_copy(
            src_ref=src,
            dst_ref=dst,
            send_sem=send_sem,
            recv_sem=recv_sem,
            device_id=device,
            device_id_type=MESH,
        )
        copy.start()
        sends.append(copy)

    def arrive(dst, send_sem, recv_sem, device):
        pltpu.make_async_remote_copy(
            src_ref=dst,
            dst_ref=dst,
            send_sem=send_sem,
            recv_sem=recv_sem,
            device_id=device,
            device_id_type=MESH,
        ).wait_recv()

    def seq_peer(k):
        return {"seq": lax.rem(s + k, n_seq)}

    for k in range(1, n_seq):
        send(xg.at[0], xg.at[k], x_send.at[k], x_recv.at[k], seq_peer(n_seq - k))

    both = jnp.concatenate([xg[0, i] for i in range(images)], axis=1)
    square = jnp.zeros((1, images * toks), F32)
    step = width // 4
    for at in range(0, width, step):
        projected = dot_first(w_in_ref[:, at : at + step], both)
        square = square + jnp.sum(projected * projected, axis=0, keepdims=True)
    inverse = lax.rsqrt(square * (1.0 / width) + 1e-06)
    rg[0] = jnp.concatenate(
        [inverse[:, i * toks : (i + 1) * toks] for i in range(images)]
        + [jnp.zeros((8 - images, toks), F32)],
        axis=0,
    )
    for k in range(1, n_seq):
        send(rg.at[0], rg.at[k], r_send.at[k], r_recv.at[k], seq_peer(n_seq - k))

    left[0:channels] = w_in_ref[...]
    scaled = split_parts(w_in_ref[...].astype(F32) * scale_ref[...])
    for at, term in enumerate(scaled):
        left[(at + 1) * channels : (at + 2) * channels] = term
    base = (PARTS + 1) * channels
    row = lax.broadcasted_iota(jnp.int32, (ROWS, width), 0)
    shift_rows = jnp.zeros((ROWS, width), F32)
    for at, term in enumerate(split_parts(shift_ref[...])):
        shift_rows = jnp.where(row == at, term.astype(F32), shift_rows)
    left[base : base + ROWS] = shift_rows.astype(BF16)

    loads[0].wait()
    loads[1].wait()
    maps = [dot(left[...], w_qkv[c]) for c in range(3)] + [dot_last(left[...], w_final[...])]
    maps = jnp.concatenate(maps, axis=1)
    total = 3 * head + channels
    plain = maps[0:channels]
    per_level = sum(maps[(at + 1) * channels : (at + 2) * channels] for at in range(PARTS))
    bias_row = jnp.sum(maps[base : base + ROWS], axis=0, keepdims=True)
    row = lax.broadcasted_iota(jnp.int32, (ROWS, total), 0)
    bias_rows = jnp.zeros((ROWS, total), F32)
    for at, term in enumerate(split_parts(bias_row)):
        bias_rows = jnp.where(row == at, term.astype(F32), bias_rows)
    bias = dot_first(bias_rows.astype(BF16), jnp.ones((ROWS, toks), BF16))
    combined = [
        jnp.concatenate(split_parts(plain + own_level(i, total) * per_level), axis=0)
        for i in range(images)
    ]

    factor = math.log2(math.e) / math.sqrt(head)
    local = []
    for k in range(n_seq):
        if k:
            arrive(xg.at[k], x_send.at[k], x_recv.at[k], seq_peer(k))
            arrive(rg.at[k], r_send.at[k], r_recv.at[k], seq_peer(k))
        rows = total if k == 0 else 3 * head
        for i in range(images):
            x = xg[k, i]
            stacked = jnp.concatenate([x] * PARTS, axis=0)
            triple = dot_first(combined[i][:, :rows], stacked) * rg[k, i : i + 1, :] + bias[:rows]
            queries[i, k] = (triple[:head] * factor).astype(BF16)
            keys[i, k * toks : (k + 1) * toks] = triple[head : 2 * head].T.astype(BF16)
            values[i, :, k * toks : (k + 1) * toks] = triple[2 * head : 3 * head].astype(BF16)
            if k == 0:
                local.append(triple[3 * head :])

    own = []
    for k in list(range(1, n_seq)) + [0]:
        for i in range(images):
            scores = dot(keys[i], queries[i, k])
            weights = jnp.exp2(scores - jnp.max(scores, axis=0, keepdims=True))
            norm = 1.0 / jnp.sum(weights, axis=0, keepdims=True)
            attended = (dot(values[i], weights.astype(BF16)) * norm).astype(BF16)
            term = dot(w_out_ref[...], attended)
            if k:
                vel_out[k, i] = term.astype(BF16)
            else:
                own.append(term)
        if k:
            send(vel_out.at[k], vel_in.at[k], vel_send.at[k], vel_recv.at[k], seq_peer(k))

    for k in range(1, n_seq):
        arrive(vel_in.at[k], vel_send.at[k], vel_recv.at[k], seq_peer(n_seq - k))
    for i in range(images):
        velocity = local[i] + own[i]
        for k in range(1, n_seq):
            velocity = velocity + vel_in[k, i].astype(F32)
        pred_ref[i] = pred_ref[i] - own_level(i, toks) * velocity
        for h in range(n_group):
            split_out[h, i] = velocity[h * ROWS : (h + 1) * ROWS].astype(BF16)

    def group_peer(k):
        return {"group": lax.rem(g + k, n_group)}

    for k in range(1, n_group):
        to = lax.rem(g + k, n_group)
        send(split_out.at[to], split_in.at[g], split_send.at[k], split_recv.at[g], group_peer(k))
    split_in[g] = split_out[g]
    for k in range(1, n_group):
        frm = lax.rem(g + k, n_group)
        arrive(split_in.at[frm], split_send.at[k], split_recv.at[frm], group_peer(k))

    part = pl.ds(pl.multiple_of(g * ROWS, ROWS), ROWS)
    sums = []
    for i in range(images):
        lv = level(i, toks)
        guided = 2.5 * split_in[1, i].astype(F32) - 1.5 * split_in[2, i].astype(F32)
        real = noisy[i, part, :] - lv * guided
        away = jnp.abs(prev_ref[i, part, :] - real)
        away = jnp.sum(jnp.sum(away, axis=0, keepdims=True), axis=1, keepdims=True)
        sums.append(jnp.broadcast_to(away, (1, 128)))
        diff[i, part, :] = (lv * (guided - split_in[3, i].astype(F32))).astype(BF16)
    dev[here] = jnp.concatenate(sums + [jnp.zeros((8 - images, 128), F32)], axis=0)
    for k in range(1, n_group):
        send(diff.at[:, part, :], diff.at[:, part, :], diff_send.at[k], diff_recv.at[g], group_peer(k))
    for dg in range(n_group):
        for ds in range(n_seq):
            if dg or ds:
                send(
                    dev.at[here],
                    dev.at[here],
                    dev_send.at[dg * n_seq + ds],
                    dev_recv.at[here],
                    {"group": lax.rem(g + dg, n_group), "seq": lax.rem(s + ds, n_seq)},
                )
    loads[2].wait()
    for k in range(1, n_group):
        frm = lax.rem(g + k, n_group)
        theirs = diff.at[:, pl.ds(pl.multiple_of(frm * ROWS, ROWS), ROWS), :]
        arrive(theirs, diff_send.at[k], diff_recv.at[frm], group_peer(k))
    products = [dot(diff[i], saved[i]) for i in range(images)]
    for dg in range(n_group):
        for ds in range(n_seq):
            if dg or ds:
                there = lax.rem(g + dg, n_group) * n_seq + lax.rem(s + ds, n_seq)
                arrive(
                    dev.at[there],
                    dev_send.at[dg * n_seq + ds],
                    dev_recv.at[there],
                    {"group": lax.rem(g + dg, n_group), "seq": lax.rem(s + ds, n_seq)},
                )
    away = dev[0]
    for at in range(1, n_group * n_seq):
        away = away + dev[at]
    spread = away * (1.0 / (n_seq * toks * channels)) + 1e-05
    gradient = 0.0
    for i in range(images):
        over = 1.0 / spread[i : i + 1, 0:1]
        gradient = gradient - products[i] * over
        dmd_ref[i] = diff[i].astype(F32) * over
    for o in range(n_plane):
        r0, c0 = (o // lane_blocks) * ROWS, (o % lane_blocks) * chunk
        grad_out[o] = gradient[r0 : r0 + ROWS, c0 : c0 + chunk].astype(BF16)

    def plane_peer(k):
        to = lax.rem(place + k, n_plane)
        return to, {"seq": to // n_dp, "dp": lax.rem(to, n_dp)}

    for k in range(1, n_plane):
        to, device = plane_peer(k)
        send(grad_out.at[to], grad_in.at[k], grad_send.at[k], grad_recv.at[k], device)
    summed = grad_out[place].astype(F32)
    for k in range(1, n_plane):
        arrive(grad_in.at[k], grad_send.at[k], grad_recv.at[k], plane_peer(n_plane - k)[1])
        summed = summed + grad_in[k].astype(F32)
    normalizer = 1.0 / math.sqrt(images * n_dp * n_seq * toks)
    gathered[place, g] = (summed * normalizer).astype(BF16)
    for k in range(1, n_group):
        send(gathered.at[place, g], gathered.at[place, g], up_send.at[k], up_recv.at[g], group_peer(k))
    for k in range(1, n_group):
        frm = lax.rem(g + k, n_group)
        arrive(gathered.at[place, frm], up_send.at[k], up_recv.at[frm], group_peer(k))
    for k in range(1, n_plane):
        to, device = plane_peer(k)
        send(gathered.at[place], gathered.at[place], all_send.at[k], all_recv.at[place], device)
    for k in range(1, n_plane):
        frm, device = plane_peer(k)
        arrive(gathered.at[frm], all_send.at[k], all_recv.at[frm], device)
    for o in range(n_plane):
        r0 = (o // lane_blocks) * ROWS
        for h in range(n_group):
            c0 = h * share + (o % lane_blocks) * chunk
            grad_ref[r0 : r0 + ROWS, c0 : c0 + chunk] = gathered[o, h].astype(F32)
    for copy in sends:
        copy.wait_send()


def fits(shape, images, toks, channels, width, head):
    n_group, n_plane = shape["group"], shape["seq"] * shape["dp"]
    row_blocks = channels // ROWS
    return (
        n_group == 4
        and channels == n_group * ROWS
        and images <= 8
        and toks % 128 == 0
        and head % 128 == 0
        and n_plane % row_blocks == 0
        and width % (n_group * (n_plane // row_blocks) * 128) == 0
    )


def per_device(
    shape,
    noise_gen,
    noise_score,
    prev_latents,
    t_idx,
    w_in,
    w_qkv,
    w_out,
    w_final,
    mod_scale,
    mod_shift,
    saved_features,
):
    images, toks, channels = noise_gen.shape
    width, head = w_in.shape[2], w_out.shape[1]
    if not fits(shape, images, toks, channels, width, head):
        return per_device_plain(
            noise_gen,
            noise_score,
            prev_latents,
            t_idx,
            w_in,
            w_qkv,
            w_out,
            w_final,
            mod_scale,
            mod_shift,
            saved_features,
        )
    n_group, n_seq, n_dp = shape["group"], shape["seq"], shape["dp"]
    n_plane = n_seq * n_dp
    share = width // n_group
    chunk = share // (n_plane // (channels // ROWS))
    vmem = pl.BlockSpec(memory_space=pltpu.VMEM)
    anywhere = pl.BlockSpec(memory_space=pl.ANY)
    dma = pltpu.SemaphoreType.DMA
    all_tokens = n_seq * toks
    total_in = n_group * n_seq
    prediction, dmd_grad, grad = pl.pallas_call(
        functools.partial(kernel, (n_group, n_seq, n_dp)),
        out_shape=(
            jax.ShapeDtypeStruct((images, channels, toks), F32),
            jax.ShapeDtypeStruct((images, channels, toks), F32),
            jax.ShapeDtypeStruct((channels, width), F32),
        ),
        in_specs=[
            pl.BlockSpec(memory_space=pltpu.SMEM),
            vmem,
            vmem,
            vmem,
            vmem,
            anywhere,
            vmem,
            anywhere,
            vmem,
            vmem,
            anywhere,
        ],
        out_specs=(vmem, vmem, vmem),
        scratch_shapes=[
            pltpu.VMEM((3, width, head), BF16),
            pltpu.VMEM((channels, width), BF16),
            pltpu.VMEM((images, toks, share), BF16),
            pltpu.VMEM(((PARTS + 1) * channels + ROWS, width), BF16),
            pltpu.VMEM((n_seq, images, channels, toks), BF16),
            pltpu.VMEM((n_seq, 8, toks), F32),
            pltpu.VMEM((images, channels, toks), F32),
            pltpu.VMEM((images, all_tokens, head), BF16),
            pltpu.VMEM((images, n_seq, head, toks), BF16),
            pltpu.VMEM((images, head, all_tokens), BF16),
            pltpu.VMEM((n_seq, images, channels, toks), BF16),
            pltpu.VMEM((n_seq, images, channels, toks), BF16),
            pltpu.VMEM((n_group, images, ROWS, toks), BF16),
            pltpu.VMEM((n_group, images, ROWS, toks), BF16),
            pltpu.VMEM((images, channels, toks), BF16),
            pltpu.VMEM((total_in, 8, 128), F32),
            pltpu.VMEM((n_plane, ROWS, chunk), BF16),
            pltpu.VMEM((n_plane, ROWS, chunk), BF16),
            pltpu.VMEM((n_plane, n_group, ROWS, chunk), BF16),
            dma((3,)),
            dma((n_seq,)),
            dma((n_seq,)),
            dma((n_seq,)),
            dma((n_seq,)),
            dma((n_seq,)),
            dma((n_seq,)),
            dma((n_group,)),
            dma((n_group,)),
            dma((n_group,)),
            dma((n_group,)),
            dma((total_in,)),
            dma((total_in,)),
            dma((n_plane,)),
            dma((n_plane,)),
            dma((n_group,)),
            dma((n_group,)),
            dma((n_plane,)),
            dma((n_plane,)),
        ],
        compiler_params=pltpu.CompilerParams(
            collective_id=0, has_side_effects=True, vmem_limit_bytes=48 * 1024 * 1024
        ),
    )(
        t_idx,
        noise_gen.transpose(0, 2, 1),
        noise_score.transpose(0, 2, 1),
        prev_latents.transpose(0, 2, 1),
        w_in[0],
        w_qkv[0].transpose(1, 0, 2),
        w_out[0].T,
        w_final[0].T,
        mod_scale,
        mod_shift,
        saved_features,
    )
    return prediction.transpose(0, 2, 1)[None], dmd_grad.transpose(0, 2, 1), grad.T


def solution(mesh):
    placed = (
        P("dp", "seq", None),
        P("dp", "seq", None),
        P("dp", "seq", None),
        P("dp"),
        P("group", None, None),
        P("group", None, None, "seq"),
        P("group", "seq", None),
        P("group", None, None),
        P("group", None),
        P("group", None),
        P("dp", "seq", None),
    )
    return jax.shard_map(
        functools.partial(per_device, dict(mesh.shape)),
        mesh=mesh,
        in_specs=placed,
        out_specs=(P("group", "dp", "seq", None), P("dp", "seq", None), P()),
        check_vma=False,
    )
```

```python
import functools
import math

import jax
import jax.numpy as jnp
from jax import lax
from jax.experimental import pallas as pl
from jax.experimental.pallas import tpu as pltpu
from jax.sharding import PartitionSpec as P

NTOK = 1024
NOISE_LEVEL_COUNT = 1000


def embed(latent, noise_level, w_in_here, scale, shift):
    projected = jnp.einsum("inp,pd->ind", latent, w_in_here, preferred_element_type=jnp.float32)
    normed = projected * lax.rsqrt(jnp.mean(projected * projected, axis=-1, keepdims=True) + 1e-06)
    return (normed * (1.0 + noise_level[:, None, None] * scale) + shift).astype(jnp.bfloat16)


def per_device_plain(
    noise_gen,
    noise_score,
    prev_latents,
    t_idx,
    w_in,
    w_qkv,
    w_out,
    w_final,
    mod_scale,
    mod_shift,
    saved_features,
):
    model_index = lax.axis_index("group")
    local_image_batch, rows_image, channels = noise_gen.shape
    width = w_in.shape[2]
    head_size = w_out.shape[1]
    level = (t_idx.astype(jnp.float32) + 0.5) / NOISE_LEVEL_COUNT
    noisy = (1.0 - level)[:, None, None] * prev_latents + level[:, None, None] * noise_score.astype(
        jnp.float32
    )
    is_generator = model_index == 0
    model_input = jnp.where(is_generator, noise_gen.astype(jnp.float32), noisy)
    noise_level = jnp.where(is_generator, jnp.ones_like(level), level)
    latent = model_input.astype(jnp.bfloat16)
    w_in_here = w_in[0]
    head_weight = w_qkv[0].reshape(width, 3 * head_size)
    scale = mod_scale[0]
    shift = mod_shift[0]
    features = embed(latent, noise_level, w_in_here, scale, shift)
    triple = jnp.einsum(
        "ind,de->ine",
        lax.all_gather(features, "seq", axis=1, tiled=True),
        head_weight,
        preferred_element_type=jnp.float32,
    ).astype(jnp.bfloat16)
    queries = triple[:, :, :head_size]
    keys = triple[:, :, head_size : 2 * head_size]
    value_rows = triple[:, :, 2 * head_size :]
    scores = jnp.einsum(
        "iqe,ike->iqk", queries, keys, preferred_element_type=jnp.float32
    ) / math.sqrt(head_size)
    probs = jax.nn.softmax(scores, axis=-1).astype(jnp.bfloat16)
    attention_result = jnp.einsum(
        "iqk,ike->iqe", probs, value_rows, preferred_element_type=jnp.float32
    ).astype(jnp.bfloat16)
    token_leading_layout = attention_result.transpose(1, 0, 2)
    output_layout = w_out[0]
    summed = (
        lax.psum_scatter(
            jnp.einsum(
                "sca,af->scf",
                token_leading_layout,
                output_layout,
                preferred_element_type=jnp.float32,
            ).astype(jnp.bfloat16),
            "seq",
            scatter_dimension=0,
            tiled=True,
        )
        .astype(jnp.float32)
        .transpose(1, 0, 2)
    )
    velocity = (
        jnp.einsum("ind,dp->inp", features, w_final[0], preferred_element_type=jnp.float32) + summed
    )
    prediction = model_input - noise_level[:, None, None] * velocity
    real_weight = jnp.where(model_index == 1, 2.5, jnp.where(model_index == 2, -1.5, 0.0))
    fake_weight = jnp.where(model_index == 3, 1.0, 0.0)
    real, fake = lax.psum((real_weight * prediction, fake_weight * prediction), "group")
    deviation = jnp.sum(jnp.abs(prev_latents - real), axis=(1, 2))
    total_dev = lax.psum(deviation, "seq")
    spread = total_dev / (NTOK * channels) + 1e-05
    dmd_grad = (fake - real) / spread[:, None, None]
    down = (-dmd_grad).astype(jnp.bfloat16)
    normalizer = 1.0 / math.sqrt(local_image_batch * lax.axis_size("dp") * NTOK)
    partial_grad = jnp.einsum(
        "ind,inp->dp", saved_features, down, preferred_element_type=jnp.float32
    )
    total_grad = lax.psum(partial_grad, ("seq", "dp"))
    return (prediction[None], dmd_grad, total_grad * normalizer)


F32 = jnp.float32
BF16 = jnp.bfloat16
MESH = pl.DeviceIdType.MESH
PARTS = 3
ROWS = 16


def dot(a, b):
    return jnp.dot(a, b, preferred_element_type=F32)


def dot_first(a, b):
    return lax.dot_general(a, b, (((0,), (0,)), ((), ())), preferred_element_type=F32)


def dot_last(a, b):
    return lax.dot_general(a, b, (((1,), (1,)), ((), ())), preferred_element_type=F32)


def split_parts(x):
    terms = []
    for _ in range(PARTS):
        term = x.astype(BF16)
        terms.append(term)
        x = x - term.astype(F32)
    return terms


def kernel(
    dims,
    t_ref,
    noise_gen_hbm,
    noise_score_hbm,
    prev_hbm,
    w_in_hbm,
    w_qkv_hbm,
    w_out_hbm,
    w_final_hbm,
    scale_hbm,
    shift_hbm,
    saved_hbm,
    pred_ref,
    dmd_ref,
    grad_ref,
    noise_gen_ref,
    noise_score_ref,
    prev_ref,
    w_in_ref,
    w_out_ref,
    scale_ref,
    shift_ref,
    w_qkv,
    w_final,
    saved,
    left,
    xg,
    rg,
    noisy,
    keys,
    queries,
    values,
    vel_out,
    vel_in,
    split_out,
    split_in,
    diff,
    dev,
    grad_out,
    grad_in,
    gathered,
    load_sem,
    x_send,
    x_recv,
    r_send,
    r_recv,
    vel_send,
    vel_recv,
    split_send,
    split_recv,
    diff_send,
    diff_recv,
    dev_send,
    dev_recv,
    grad_send,
    grad_recv,
    up_send,
    up_recv,
    all_send,
    core_send,
    all_recv,
):
    n_group, n_seq, n_dp = dims
    n_plane = n_seq * n_dp
    images, channels, toks = prev_ref.shape
    width = w_in_ref.shape[1]
    n_same = n_plane // 2
    head = w_out_ref.shape[1]
    share = saved.shape[2]
    chunk = grad_in.shape[2]
    lane_blocks = share // chunk
    g = lax.axis_index("group")
    s = lax.axis_index("seq")
    d = lax.axis_index("dp")
    here = g * n_seq + s
    place = s * n_dp + d

    saved_part = saved_hbm.at[:, :, pl.ds(pl.multiple_of(g * share, 128), share)]
    pairs = [
        (noise_gen_hbm, noise_gen_ref),
        (noise_score_hbm, noise_score_ref),
        (prev_hbm, prev_ref),
        (w_in_hbm, w_in_ref),
        (scale_hbm, scale_ref),
        (shift_hbm, shift_ref),
        (w_qkv_hbm, w_qkv),
        (w_final_hbm, w_final),
        (w_out_hbm, w_out_ref),
        (saved_part, saved),
    ]
    loads = [pltpu.make_async_copy(src, dst, load_sem.at[at]) for at, (src, dst) in enumerate(pairs)]
    for load in loads:
        load.start()

    barrier = pltpu.get_barrier_semaphore()
    peers = 0
    for dg in range(n_group):
        for ds in range(n_seq):
            if dg or ds:
                pl.semaphore_signal(
                    barrier,
                    inc=1,
                    device_id={"group": lax.rem(g + dg, n_group), "seq": lax.rem(s + ds, n_seq)},
                    device_id_type=MESH,
                )
                peers += 1
    for ds in range(n_seq):
        for dd in range(1, n_dp):
            pl.semaphore_signal(
                barrier,
                inc=1,
                device_id={"seq": lax.rem(s + ds, n_seq), "dp": lax.rem(d + dd, n_dp)},
                device_id_type=MESH,
            )
            peers += 1

    generator = jnp.where(g == 0, 1.0, 0.0).astype(F32)

    def level(i, lanes):
        return (jnp.full((1, lanes), t_ref[i].astype(F32), F32) + 0.5) / NOISE_LEVEL_COUNT

    def own_level(i, lanes):
        return generator + (1.0 - generator) * level(i, lanes)

    for load in loads[:3]:
        load.wait()
    for i in range(images):
        lv = level(i, toks)
        noisy[i] = (1.0 - lv) * prev_ref[i] + lv * noise_score_ref[i].astype(F32)
        model_input = generator * noise_gen_ref[i].astype(F32) + (1.0 - generator) * noisy[i]
        pred_ref[i] = model_input
        xg[0, i] = model_input.astype(BF16)

    pl.semaphore_wait(barrier, peers)

    sends = []

    def send(src, dst, send_sem, recv_sem, device):
        copy = pltpu.make_async_remote_copy(
            src_ref=src,
            dst_ref=dst,
            send_sem=send_sem,
            recv_sem=recv_sem,
            device_id=device,
            device_id_type=MESH,
        )
        copy.start()
        sends.append(copy)

    def arrive(dst, send_sem, recv_sem, device):
        pltpu.make_async_remote_copy(
            src_ref=dst,
            dst_ref=dst,
            send_sem=send_sem,
            recv_sem=recv_sem,
            device_id=device,
            device_id_type=MESH,
        ).wait_recv()

    def seq_peer(k):
        return {"seq": lax.rem(s + k, n_seq)}

    for k in range(1, n_seq):
        send(xg.at[0], xg.at[k], x_send.at[k], x_recv.at[k], seq_peer(n_seq - k))

    for load in loads[3:6]:
        load.wait()
    both = jnp.concatenate([xg[0, i] for i in range(images)], axis=1)
    square = jnp.zeros((1, images * toks), F32)
    step = width // 4
    for at in range(0, width, step):
        projected = dot_first(w_in_ref[:, at : at + step], both)
        square = square + jnp.sum(projected * projected, axis=0, keepdims=True)
    inverse = lax.rsqrt(square * (1.0 / width) + 1e-06)
    rg[0] = jnp.concatenate(
        [inverse[:, i * toks : (i + 1) * toks] for i in range(images)]
        + [jnp.zeros((8 - images, toks), F32)],
        axis=0,
    )
    for k in range(1, n_seq):
        send(rg.at[0], rg.at[k], r_send.at[k], r_recv.at[k], seq_peer(n_seq - k))

    left[0:channels] = w_in_ref[...]
    scaled = split_parts(w_in_ref[...].astype(F32) * scale_ref[...])
    for at, term in enumerate(scaled):
        left[(at + 1) * channels : (at + 2) * channels] = term
    base = (PARTS + 1) * channels
    row = lax.broadcasted_iota(jnp.int32, (ROWS, width), 0)
    shift_rows = jnp.zeros((ROWS, width), F32)
    for at, term in enumerate(split_parts(shift_ref[...])):
        shift_rows = jnp.where(row == at, term.astype(F32), shift_rows)
    left[base : base + ROWS] = shift_rows.astype(BF16)

    for load in loads[6:9]:
        load.wait()
    maps = [dot(left[...], w_qkv[c]) for c in range(3)] + [dot_last(left[...], w_final[...])]
    maps = jnp.concatenate(maps, axis=1)
    total = 3 * head + channels
    plain = maps[0:channels]
    per_level = sum(maps[(at + 1) * channels : (at + 2) * channels] for at in range(PARTS))
    bias_row = jnp.sum(maps[base : base + ROWS], axis=0, keepdims=True)
    row = lax.broadcasted_iota(jnp.int32, (ROWS, total), 0)
    bias_rows = jnp.zeros((ROWS, total), F32)
    for at, term in enumerate(split_parts(bias_row)):
        bias_rows = jnp.where(row == at, term.astype(F32), bias_rows)
    bias = dot_first(bias_rows.astype(BF16), jnp.ones((ROWS, toks), BF16))
    combined = [
        jnp.concatenate(split_parts(plain + own_level(i, total) * per_level), axis=0)
        for i in range(images)
    ]

    factor = math.log2(math.e) / math.sqrt(head)
    local = []
    for k in range(n_seq):
        if k:
            arrive(xg.at[k], x_send.at[k], x_recv.at[k], seq_peer(k))
            arrive(rg.at[k], r_send.at[k], r_recv.at[k], seq_peer(k))
        rows = total if k == 0 else 3 * head
        for i in range(images):
            x = xg[k, i]
            stacked = jnp.concatenate([x] * PARTS, axis=0)
            triple = dot_first(combined[i][:, :rows], stacked) * rg[k, i : i + 1, :] + bias[:rows]
            queries[i, k] = (triple[:head] * factor).astype(BF16)
            keys[i, k * toks : (k + 1) * toks] = triple[head : 2 * head].T.astype(BF16)
            values[i, :, k * toks : (k + 1) * toks] = triple[2 * head : 3 * head].astype(BF16)
            if k == 0:
                local.append(triple[3 * head :])

    own = []
    for k in list(range(1, n_seq)) + [0]:
        for i in range(images):
            scores = dot(keys[i], queries[i, k])
            weights = jnp.exp2(scores - jnp.max(scores, axis=0, keepdims=True))
            norm = 1.0 / jnp.sum(weights, axis=0, keepdims=True)
            attended = (dot(values[i], weights.astype(BF16)) * norm).astype(BF16)
            term = dot(w_out_ref[...], attended)
            if k:
                vel_out[k, i] = term.astype(BF16)
            else:
                own.append(term)
        if k:
            send(vel_out.at[k], vel_in.at[k], vel_send.at[k], vel_recv.at[k], seq_peer(k))

    for k in range(1, n_seq):
        arrive(vel_in.at[k], vel_send.at[k], vel_recv.at[k], seq_peer(n_seq - k))
    for i in range(images):
        velocity = local[i] + own[i]
        for k in range(1, n_seq):
            velocity = velocity + vel_in[k, i].astype(F32)
        pred_ref[i] = pred_ref[i] - own_level(i, toks) * velocity
        for h in range(n_group):
            split_out[h, i] = velocity[h * ROWS : (h + 1) * ROWS].astype(BF16)

    def group_peer(k):
        return {"group": lax.rem(g + k, n_group)}

    for k in range(1, n_group):
        to = lax.rem(g + k, n_group)
        send(split_out.at[to], split_in.at[g], split_send.at[k], split_recv.at[g], group_peer(k))
    split_in[g] = split_out[g]
    for k in range(1, n_group):
        frm = lax.rem(g + k, n_group)
        arrive(split_in.at[frm], split_send.at[k], split_recv.at[frm], group_peer(k))

    part = pl.ds(pl.multiple_of(g * ROWS, ROWS), ROWS)
    sums = []
    for i in range(images):
        lv = level(i, toks)
        guided = 2.5 * split_in[1, i].astype(F32) - 1.5 * split_in[2, i].astype(F32)
        real = noisy[i, part, :] - lv * guided
        away = jnp.abs(prev_ref[i, part, :] - real)
        away = jnp.sum(jnp.sum(away, axis=0, keepdims=True), axis=1, keepdims=True)
        sums.append(jnp.broadcast_to(away, (1, 128)))
        diff[i, part, :] = (lv * (guided - split_in[3, i].astype(F32))).astype(BF16)
    dev[here] = jnp.concatenate(sums + [jnp.zeros((8 - images, 128), F32)], axis=0)
    for k in range(1, n_group):
        send(diff.at[:, part, :], diff.at[:, part, :], diff_send.at[k], diff_recv.at[g], group_peer(k))
    for dg in range(n_group):
        for ds in range(n_seq):
            if dg or ds:
                send(
                    dev.at[here],
                    dev.at[here],
                    dev_send.at[dg * n_seq + ds],
                    dev_recv.at[here],
                    {"group": lax.rem(g + dg, n_group), "seq": lax.rem(s + ds, n_seq)},
                )
    loads[9].wait()
    for k in range(1, n_group):
        frm = lax.rem(g + k, n_group)
        theirs = diff.at[:, pl.ds(pl.multiple_of(frm * ROWS, ROWS), ROWS), :]
        arrive(theirs, diff_send.at[k], diff_recv.at[frm], group_peer(k))
    products = [dot(diff[i], saved[i]) for i in range(images)]
    for dg in range(n_group):
        for ds in range(n_seq):
            if dg or ds:
                there = lax.rem(g + dg, n_group) * n_seq + lax.rem(s + ds, n_seq)
                arrive(
                    dev.at[there],
                    dev_send.at[dg * n_seq + ds],
                    dev_recv.at[there],
                    {"group": lax.rem(g + dg, n_group), "seq": lax.rem(s + ds, n_seq)},
                )
    away = dev[0]
    for at in range(1, n_group * n_seq):
        away = away + dev[at]
    spread = away * (1.0 / (n_seq * toks * channels)) + 1e-05
    gradient = 0.0
    for i in range(images):
        over = 1.0 / spread[i : i + 1, 0:1]
        gradient = gradient - products[i] * over
        dmd_ref[i] = diff[i].astype(F32) * over
    for o in range(n_plane):
        r0, c0 = (o // lane_blocks) * ROWS, (o % lane_blocks) * chunk
        grad_out[o] = gradient[r0 : r0 + ROWS, c0 : c0 + chunk].astype(BF16)

    def plane_peer(k):
        to = lax.rem(place + k, n_plane)
        return to, {"seq": to // n_dp, "dp": lax.rem(to, n_dp)}

    for k in range(1, n_plane):
        to, device = plane_peer(k)
        send(grad_out.at[to], grad_in.at[k], grad_send.at[k], grad_recv.at[k], device)
    summed = grad_out[place].astype(F32)
    for k in range(1, n_plane):
        arrive(grad_in.at[k], grad_send.at[k], grad_recv.at[k], plane_peer(n_plane - k)[1])
        summed = summed + grad_in[k].astype(F32)
    normalizer = 1.0 / math.sqrt(images * n_dp * n_seq * toks)
    gathered[place, g] = (summed * normalizer).astype(BF16)
    other_core = {"seq": s + 1 - 2 * lax.rem(s, 2)}

    def same_core(k):
        seq, dp = lax.rem(s + 2 * (k // n_dp), n_seq), lax.rem(d + k % n_dp, n_dp)
        return seq * n_dp + dp, {"seq": seq, "dp": dp}

    def pass_on(h, turn):
        for k in range(1, n_same):
            at = gathered.at[place, h]
            send(at, at, all_send.at[k, turn], all_recv.at[place, h], same_core(k)[1])
        at = gathered.at[place, h]
        send(at, at, core_send.at[0, turn], all_recv.at[place, h], other_core)

    for k in range(1, n_group):
        at = gathered.at[place, g]
        send(at, at, up_send.at[k], up_recv.at[g], group_peer(k))
    pass_on(g, 0)
    for k in range(1, n_group):
        frm = lax.rem(g + k, n_group)
        arrive(gathered.at[place, frm], up_send.at[k], up_recv.at[frm], group_peer(k))
        pass_on(frm, k)
    for turn in range(n_group):
        h = lax.rem(g + turn, n_group)
        for k in range(1, n_same):
            frm, device = same_core(k)
            at = gathered.at[frm, h]
            arrive(at, all_send.at[k, turn], all_recv.at[frm, h], device)
            send(at, at, core_send.at[k, turn], all_recv.at[frm, h], other_core)
    for turn in range(n_group):
        h = lax.rem(g + turn, n_group)
        for k in range(n_same):
            frm = same_core(k)[0] + n_dp - 2 * n_dp * lax.rem(s, 2)
            arrive(gathered.at[frm, h], core_send.at[k, turn], all_recv.at[frm, h], other_core)
    for o in range(n_plane):
        r0 = (o // lane_blocks) * ROWS
        for h in range(n_group):
            c0 = h * share + (o % lane_blocks) * chunk
            grad_ref[r0 : r0 + ROWS, c0 : c0 + chunk] = gathered[o, h].astype(F32)
    for copy in sends:
        copy.wait_send()


def fits(shape, images, toks, channels, width, head):
    n_group, n_plane = shape["group"], shape["seq"] * shape["dp"]
    row_blocks = channels // ROWS
    return (
        n_group == 4
        and channels == n_group * ROWS
        and images <= 8
        and toks % 128 == 0
        and head % 128 == 0
        and shape["seq"] % 2 == 0
        and n_plane % row_blocks == 0
        and width % (n_group * (n_plane // row_blocks) * 128) == 0
    )


def per_device(
    shape,
    noise_gen,
    noise_score,
    prev_latents,
    t_idx,
    w_in,
    w_qkv,
    w_out,
    w_final,
    mod_scale,
    mod_shift,
    saved_features,
):
    images, toks, channels = noise_gen.shape
    width, head = w_in.shape[2], w_out.shape[1]
    if not fits(shape, images, toks, channels, width, head):
        return per_device_plain(
            noise_gen,
            noise_score,
            prev_latents,
            t_idx,
            w_in,
            w_qkv,
            w_out,
            w_final,
            mod_scale,
            mod_shift,
            saved_features,
        )
    n_group, n_seq, n_dp = shape["group"], shape["seq"], shape["dp"]
    n_plane = n_seq * n_dp
    share = width // n_group
    chunk = share // (n_plane // (channels // ROWS))
    vmem = pl.BlockSpec(memory_space=pltpu.VMEM)
    hbm = pl.BlockSpec(memory_space=pltpu.HBM)
    dma = pltpu.SemaphoreType.DMA
    all_tokens = n_seq * toks
    total_in = n_group * n_seq
    prediction, dmd_grad, grad = pl.pallas_call(
        functools.partial(kernel, (n_group, n_seq, n_dp)),
        out_shape=(
            jax.ShapeDtypeStruct((images, channels, toks), F32),
            jax.ShapeDtypeStruct((images, channels, toks), F32),
            jax.ShapeDtypeStruct((channels, width), F32),
        ),
        in_specs=[pl.BlockSpec(memory_space=pltpu.SMEM)] + [hbm] * 10,
        out_specs=(vmem, vmem, vmem),
        scratch_shapes=[
            pltpu.VMEM((images, channels, toks), BF16),
            pltpu.VMEM((images, channels, toks), BF16),
            pltpu.VMEM((images, channels, toks), F32),
            pltpu.VMEM((channels, width), BF16),
            pltpu.VMEM((channels, head), BF16),
            pltpu.VMEM((1, width), F32),
            pltpu.VMEM((1, width), F32),
            pltpu.VMEM((3, width, head), BF16),
            pltpu.VMEM((channels, width), BF16),
            pltpu.VMEM((images, toks, share), BF16),
            pltpu.VMEM(((PARTS + 1) * channels + ROWS, width), BF16),
            pltpu.VMEM((n_seq, images, channels, toks), BF16),
            pltpu.VMEM((n_seq, 8, toks), F32),
            pltpu.VMEM((images, channels, toks), F32),
            pltpu.VMEM((images, all_tokens, head), BF16),
            pltpu.VMEM((images, n_seq, head, toks), BF16),
            pltpu.VMEM((images, head, all_tokens), BF16),
            pltpu.VMEM((n_seq, images, channels, toks), BF16),
            pltpu.VMEM((n_seq, images, channels, toks), BF16),
            pltpu.VMEM((n_group, images, ROWS, toks), BF16),
            pltpu.VMEM((n_group, images, ROWS, toks), BF16),
            pltpu.VMEM((images, channels, toks), BF16),
            pltpu.VMEM((total_in, 8, 128), F32),
            pltpu.VMEM((n_plane, ROWS, chunk), BF16),
            pltpu.VMEM((n_plane, ROWS, chunk), BF16),
            pltpu.VMEM((n_plane, n_group, ROWS, chunk), BF16),
            dma((10,)),
            dma((n_seq,)),
            dma((n_seq,)),
            dma((n_seq,)),
            dma((n_seq,)),
            dma((n_seq,)),
            dma((n_seq,)),
            dma((n_group,)),
            dma((n_group,)),
            dma((n_group,)),
            dma((n_group,)),
            dma((total_in,)),
            dma((total_in,)),
            dma((n_plane,)),
            dma((n_plane,)),
            dma((n_group,)),
            dma((n_group,)),
            dma((n_plane // 2, n_group)),
            dma((n_plane // 2, n_group)),
            dma((n_plane, n_group)),
        ],
        compiler_params=pltpu.CompilerParams(
            collective_id=0, has_side_effects=True, vmem_limit_bytes=60 * 1024 * 1024
        ),
    )(
        t_idx,
        noise_gen.transpose(0, 2, 1),
        noise_score.transpose(0, 2, 1),
        prev_latents.transpose(0, 2, 1),
        w_in[0],
        w_qkv[0].transpose(1, 0, 2),
        w_out[0].T,
        w_final[0].T,
        mod_scale,
        mod_shift,
        saved_features,
    )
    return prediction.transpose(0, 2, 1)[None], dmd_grad.transpose(0, 2, 1), grad.T


def solution(mesh):
    placed = (
        P("dp", "seq", None),
        P("dp", "seq", None),
        P("dp", "seq", None),
        P("dp"),
        P("group", None, None),
        P("group", None, None, "seq"),
        P("group", "seq", None),
        P("group", None, None),
        P("group", None),
        P("group", None),
        P("dp", "seq", None),
    )
    return jax.shard_map(
        functools.partial(per_device, dict(mesh.shape)),
        mesh=mesh,
        in_specs=placed,
        out_specs=(P("group", "dp", "seq", None), P("dp", "seq", None), P()),
        check_vma=False,
    )
```

```python
import functools
import math

import jax
import jax.numpy as jnp
from jax import lax
from jax.experimental import pallas as pl
from jax.experimental.pallas import tpu as pltpu
from jax.sharding import PartitionSpec as P

NTOK = 1024
NOISE_LEVEL_COUNT = 1000


def embed(latent, noise_level, w_in_here, scale, shift):
    projected = jnp.einsum("inp,pd->ind", latent, w_in_here, preferred_element_type=jnp.float32)
    normed = projected * lax.rsqrt(jnp.mean(projected * projected, axis=-1, keepdims=True) + 1e-06)
    return (normed * (1.0 + noise_level[:, None, None] * scale) + shift).astype(jnp.bfloat16)


def per_device_plain(
    noise_gen,
    noise_score,
    prev_latents,
    t_idx,
    w_in,
    w_qkv,
    w_out,
    w_final,
    mod_scale,
    mod_shift,
    saved_features,
):
    model_index = lax.axis_index("group")
    local_image_batch, rows_image, channels = noise_gen.shape
    width = w_in.shape[2]
    head_size = w_out.shape[1]
    level = (t_idx.astype(jnp.float32) + 0.5) / NOISE_LEVEL_COUNT
    noisy = (1.0 - level)[:, None, None] * prev_latents + level[:, None, None] * noise_score.astype(
        jnp.float32
    )
    is_generator = model_index == 0
    model_input = jnp.where(is_generator, noise_gen.astype(jnp.float32), noisy)
    noise_level = jnp.where(is_generator, jnp.ones_like(level), level)
    latent = model_input.astype(jnp.bfloat16)
    w_in_here = w_in[0]
    head_weight = w_qkv[0].reshape(width, 3 * head_size)
    scale = mod_scale[0]
    shift = mod_shift[0]
    features = embed(latent, noise_level, w_in_here, scale, shift)
    triple = jnp.einsum(
        "ind,de->ine",
        lax.all_gather(features, "seq", axis=1, tiled=True),
        head_weight,
        preferred_element_type=jnp.float32,
    ).astype(jnp.bfloat16)
    queries = triple[:, :, :head_size]
    keys = triple[:, :, head_size : 2 * head_size]
    value_rows = triple[:, :, 2 * head_size :]
    scores = jnp.einsum(
        "iqe,ike->iqk", queries, keys, preferred_element_type=jnp.float32
    ) / math.sqrt(head_size)
    probs = jax.nn.softmax(scores, axis=-1).astype(jnp.bfloat16)
    attention_result = jnp.einsum(
        "iqk,ike->iqe", probs, value_rows, preferred_element_type=jnp.float32
    ).astype(jnp.bfloat16)
    token_leading_layout = attention_result.transpose(1, 0, 2)
    output_layout = w_out[0]
    summed = (
        lax.psum_scatter(
            jnp.einsum(
                "sca,af->scf",
                token_leading_layout,
                output_layout,
                preferred_element_type=jnp.float32,
            ).astype(jnp.bfloat16),
            "seq",
            scatter_dimension=0,
            tiled=True,
        )
        .astype(jnp.float32)
        .transpose(1, 0, 2)
    )
    velocity = (
        jnp.einsum("ind,dp->inp", features, w_final[0], preferred_element_type=jnp.float32) + summed
    )
    prediction = model_input - noise_level[:, None, None] * velocity
    real_weight = jnp.where(model_index == 1, 2.5, jnp.where(model_index == 2, -1.5, 0.0))
    fake_weight = jnp.where(model_index == 3, 1.0, 0.0)
    real, fake = lax.psum((real_weight * prediction, fake_weight * prediction), "group")
    deviation = jnp.sum(jnp.abs(prev_latents - real), axis=(1, 2))
    total_dev = lax.psum(deviation, "seq")
    spread = total_dev / (NTOK * channels) + 1e-05
    dmd_grad = (fake - real) / spread[:, None, None]
    down = (-dmd_grad).astype(jnp.bfloat16)
    normalizer = 1.0 / math.sqrt(local_image_batch * lax.axis_size("dp") * NTOK)
    partial_grad = jnp.einsum(
        "ind,inp->dp", saved_features, down, preferred_element_type=jnp.float32
    )
    total_grad = lax.psum(partial_grad, ("seq", "dp"))
    return (prediction[None], dmd_grad, total_grad * normalizer)


F32 = jnp.float32
BF16 = jnp.bfloat16
MESH = pl.DeviceIdType.MESH
PARTS = 3
ROWS = 16


def dot(a, b):
    return jnp.dot(a, b, preferred_element_type=F32)


def dot_first(a, b):
    return lax.dot_general(a, b, (((0,), (0,)), ((), ())), preferred_element_type=F32)


def dot_last(a, b):
    return lax.dot_general(a, b, (((1,), (1,)), ((), ())), preferred_element_type=F32)


def split_parts(x):
    terms = []
    for _ in range(PARTS):
        term = x.astype(BF16)
        terms.append(term)
        x = x - term.astype(F32)
    return terms


def kernel(
    dims,
    t_hbm,
    noise_gen_hbm,
    noise_score_hbm,
    prev_hbm,
    w_in_hbm,
    w_qkv_hbm,
    w_out_hbm,
    w_final_hbm,
    scale_hbm,
    shift_hbm,
    saved_hbm,
    pred_ref,
    dmd_ref,
    grad_ref,
    noise_gen_ref,
    noise_score_ref,
    prev_ref,
    w_in_ref,
    w_out_ref,
    scale_ref,
    shift_ref,
    t_ref,
    w_qkv,
    w_final,
    saved,
    left,
    xg,
    rg,
    noisy,
    keys,
    queries,
    values,
    vel_out,
    vel_in,
    split_out,
    split_in,
    diff,
    dev,
    grad_out,
    grad_in,
    gathered,
    load_sem,
    x_send,
    x_recv,
    r_send,
    r_recv,
    vel_send,
    vel_recv,
    split_send,
    split_recv,
    diff_send,
    diff_recv,
    dev_send,
    dev_recv,
    grad_send,
    grad_recv,
    up_send,
    up_recv,
    all_send,
    core_send,
    all_recv,
):
    n_group, n_seq, n_dp = dims
    n_plane = n_seq * n_dp
    images, channels, toks = prev_ref.shape
    width = w_in_ref.shape[1]
    n_same = n_plane // 2
    head = w_out_ref.shape[1]
    chunk = grad_in.shape[3]
    g = lax.axis_index("group")
    s = lax.axis_index("seq")
    d = lax.axis_index("dp")
    place = s * n_dp + d
    here = g * n_plane + place

    pairs = [
        (noise_gen_hbm, noise_gen_ref),
        (noise_score_hbm, noise_score_ref),
        (prev_hbm, prev_ref),
        (w_in_hbm, w_in_ref),
        (scale_hbm, scale_ref),
        (shift_hbm, shift_ref),
        (w_final_hbm, w_final),
        (w_out_hbm, w_out_ref),
    ]
    pairs += [(w_qkv_hbm.at[c], w_qkv.at[:, c * head : (c + 1) * head]) for c in range(3)]
    pairs += [(saved_hbm, saved), (t_hbm, t_ref)]
    loads = [pltpu.make_async_copy(src, dst, load_sem.at[at]) for at, (src, dst) in enumerate(pairs)]
    for load in loads:
        load.start()

    barrier = pltpu.get_barrier_semaphore()
    others = [
        (dg, ds, dd)
        for dg in range(n_group)
        for ds in range(n_seq)
        for dd in range(n_dp)
        if dg or ds or dd
    ]

    def other(dg, ds, dd):
        gg, ss, dp = lax.rem(g + dg, n_group), lax.rem(s + ds, n_seq), lax.rem(d + dd, n_dp)
        return (gg * n_seq + ss) * n_dp + dp, {"group": gg, "seq": ss, "dp": dp}

    for shift in others:
        pl.semaphore_signal(barrier, inc=1, device_id=other(*shift)[1], device_id_type=MESH)

    generator = jnp.where(g == 0, 1.0, 0.0).astype(F32)

    def level(i, lanes):
        return (jnp.full((1, lanes), t_ref[i].astype(F32), F32) + 0.5) / NOISE_LEVEL_COUNT

    def own_level(i, lanes):
        return generator + (1.0 - generator) * level(i, lanes)

    for load in loads[:3] + loads[12:]:
        load.wait()
    for i in range(images):
        lv = level(i, toks)
        noisy[i] = (1.0 - lv) * prev_ref[i] + lv * noise_score_ref[i].astype(F32)
        model_input = generator * noise_gen_ref[i].astype(F32) + (1.0 - generator) * noisy[i]
        pred_ref[i] = model_input
        xg[0, i] = model_input.astype(BF16)

    pl.semaphore_wait(barrier, len(others))

    sends = []

    def send(src, dst, send_sem, recv_sem, device):
        copy = pltpu.make_async_remote_copy(
            src_ref=src,
            dst_ref=dst,
            send_sem=send_sem,
            recv_sem=recv_sem,
            device_id=device,
            device_id_type=MESH,
        )
        copy.start()
        sends.append(copy)

    def arrive(dst, send_sem, recv_sem, device):
        pltpu.make_async_remote_copy(
            src_ref=dst,
            dst_ref=dst,
            send_sem=send_sem,
            recv_sem=recv_sem,
            device_id=device,
            device_id_type=MESH,
        ).wait_recv()

    def seq_peer(k):
        return {"seq": lax.rem(s + k, n_seq)}

    for k in range(1, n_seq):
        send(xg.at[0], xg.at[k], x_send.at[k], x_recv.at[k], seq_peer(n_seq - k))

    for load in loads[3:6]:
        load.wait()
    both = jnp.concatenate([xg[0, i] for i in range(images)], axis=1)
    square = jnp.zeros((1, images * toks), F32)
    step = width // 4
    for at in range(0, width, step):
        projected = dot_first(w_in_ref[:, at : at + step], both)
        square = square + jnp.sum(projected * projected, axis=0, keepdims=True)
    inverse = lax.rsqrt(square * (1.0 / width) + 1e-06)
    rg[0] = jnp.concatenate(
        [inverse[:, i * toks : (i + 1) * toks] for i in range(images)]
        + [jnp.zeros((8 - images, toks), F32)],
        axis=0,
    )
    for k in range(1, n_seq):
        send(rg.at[0], rg.at[k], r_send.at[k], r_recv.at[k], seq_peer(n_seq - k))

    left[0:channels] = w_in_ref[...]
    scaled = split_parts(w_in_ref[...].astype(F32) * scale_ref[...])
    for at, term in enumerate(scaled):
        left[(at + 1) * channels : (at + 2) * channels] = term
    base = (PARTS + 1) * channels
    row = lax.broadcasted_iota(jnp.int32, (ROWS, width), 0)
    shift_rows = jnp.zeros((ROWS, width), F32)
    for at, term in enumerate(split_parts(shift_ref[...])):
        shift_rows = jnp.where(row == at, term.astype(F32), shift_rows)
    left[base : base + ROWS] = shift_rows.astype(BF16)

    for load in loads[6:11]:
        load.wait()
    maps = jnp.concatenate([dot(left[...], w_qkv[...]), dot_last(left[...], w_final[...])], axis=1)
    total = 3 * head + channels
    plain = maps[0:channels]
    per_level = sum(maps[(at + 1) * channels : (at + 2) * channels] for at in range(PARTS))
    bias_row = jnp.sum(maps[base : base + ROWS], axis=0, keepdims=True)
    row = lax.broadcasted_iota(jnp.int32, (ROWS, total), 0)
    bias_rows = jnp.zeros((ROWS, total), F32)
    for at, term in enumerate(split_parts(bias_row)):
        bias_rows = jnp.where(row == at, term.astype(F32), bias_rows)
    bias = dot_first(bias_rows.astype(BF16), jnp.ones((ROWS, toks), BF16))
    combined = [
        jnp.concatenate(split_parts(plain + own_level(i, total) * per_level), axis=0)
        for i in range(images)
    ]

    factor = math.log2(math.e) / math.sqrt(head)
    local = []
    for k in range(n_seq):
        if k:
            arrive(xg.at[k], x_send.at[k], x_recv.at[k], seq_peer(k))
            arrive(rg.at[k], r_send.at[k], r_recv.at[k], seq_peer(k))
        rows = total if k == 0 else 3 * head
        for i in range(images):
            x = xg[k, i]
            stacked = jnp.concatenate([x] * PARTS, axis=0)
            triple = dot_first(combined[i][:, :rows], stacked) * rg[k, i : i + 1, :] + bias[:rows]
            queries[i, k] = (triple[:head] * factor).astype(BF16)
            keys[i, k * toks : (k + 1) * toks] = triple[head : 2 * head].T.astype(BF16)
            values[i, :, k * toks : (k + 1) * toks] = triple[2 * head : 3 * head].astype(BF16)
            if k == 0:
                local.append(triple[3 * head :])

    own = []
    for k in list(range(1, n_seq)) + [0]:
        for i in range(images):
            scores = dot(keys[i], queries[i, k])
            weights = jnp.exp2(scores - jnp.max(scores, axis=0, keepdims=True))
            norm = 1.0 / jnp.sum(weights, axis=0, keepdims=True)
            attended = (dot(values[i], weights.astype(BF16)) * norm).astype(BF16)
            term = dot(w_out_ref[...], attended)
            if k:
                vel_out[k, i] = term.astype(BF16)
            else:
                own.append(term)
        if k:
            send(vel_out.at[k], vel_in.at[k], vel_send.at[k], vel_recv.at[k], seq_peer(k))

    for k in range(1, n_seq):
        arrive(vel_in.at[k], vel_send.at[k], vel_recv.at[k], seq_peer(n_seq - k))
    for i in range(images):
        velocity = local[i] + own[i]
        for k in range(1, n_seq):
            velocity = velocity + vel_in[k, i].astype(F32)
        pred_ref[i] = pred_ref[i] - own_level(i, toks) * velocity
        for h in range(n_group):
            split_out[h, i] = velocity[h * ROWS : (h + 1) * ROWS].astype(BF16)

    def group_peer(k):
        return {"group": lax.rem(g + k, n_group)}

    for k in range(1, n_group):
        to = lax.rem(g + k, n_group)
        send(split_out.at[to], split_in.at[g], split_send.at[k], split_recv.at[g], group_peer(k))
    split_in[g] = split_out[g]
    for k in range(1, n_group):
        frm = lax.rem(g + k, n_group)
        arrive(split_in.at[frm], split_send.at[k], split_recv.at[frm], group_peer(k))

    part = pl.ds(pl.multiple_of(g * ROWS, ROWS), ROWS)
    sums, mine = [], []
    for i in range(images):
        lv = level(i, toks)
        guided = 2.5 * split_in[1, i].astype(F32) - 1.5 * split_in[2, i].astype(F32)
        real = noisy[i, part, :] - lv * guided
        away = jnp.abs(prev_ref[i, part, :] - real)
        away = jnp.sum(jnp.sum(away, axis=0, keepdims=True), axis=1, keepdims=True)
        sums.append(jnp.broadcast_to(away, (1, 128)))
        mine.append((lv * (guided - split_in[3, i].astype(F32))).astype(BF16))
        diff[i, part, :] = mine[i]
    dev[here] = jnp.concatenate(sums + [jnp.zeros((8 - images, 128), F32)], axis=0)
    for at, shift in enumerate(others):
        send(dev.at[here], dev.at[here], dev_send.at[at], dev_recv.at[here], other(*shift)[1])
    loads[11].wait()
    for i in range(images):
        product = dot(mine[i], saved[i])
        for o in range(n_plane):
            grad_out[o, i] = product[:, o * chunk : (o + 1) * chunk].astype(BF16)

    def plane_peer(k):
        to = lax.rem(place + k, n_plane)
        return to, {"seq": to // n_dp, "dp": lax.rem(to, n_dp)}

    for k in range(1, n_plane):
        to, device = plane_peer(k)
        send(grad_out.at[to], grad_in.at[place], grad_send.at[k], grad_recv.at[place], device)
    grad_in[place] = grad_out[place]
    for k in range(1, n_group):
        at = diff.at[:, part, :]
        send(at, at, diff_send.at[k], diff_recv.at[g], group_peer(k))
    for at, shift in enumerate(others):
        there, device = other(*shift)
        arrive(dev.at[there], dev_send.at[at], dev_recv.at[there], device)
    over = []
    for dd in range(n_dp):
        away = dev[dd]
        for at in range(1, n_group * n_seq):
            away = away + dev[at * n_dp + dd]
        over.append(1.0 / (away * (1.0 / (n_seq * toks * channels)) + 1e-05))
    for k in range(1, n_plane):
        frm, device = plane_peer(k)
        arrive(grad_in.at[frm], grad_send.at[k], grad_recv.at[frm], device)
    normalizer = 1.0 / math.sqrt(images * n_dp * n_seq * toks)
    summed = jnp.zeros((ROWS, chunk), F32)
    for o in range(n_plane):
        for i in range(images):
            weight = over[o % n_dp][i : i + 1, 0:1] * -normalizer
            summed = summed + grad_in[o, i].astype(F32) * weight
    gathered[place, g] = summed.astype(BF16)
    other_core = {"seq": s + 1 - 2 * lax.rem(s, 2)}

    def same_core(k):
        seq, dp = lax.rem(s + 2 * (k // n_dp), n_seq), lax.rem(d + k % n_dp, n_dp)
        return seq * n_dp + dp, {"seq": seq, "dp": dp}

    def pass_on(h, turn):
        for k in range(1, n_same):
            at = gathered.at[place, h]
            send(at, at, all_send.at[k, turn], all_recv.at[place, h], same_core(k)[1])
        at = gathered.at[place, h]
        send(at, at, core_send.at[0, turn], all_recv.at[place, h], other_core)

    for k in range(1, n_group):
        at = gathered.at[place, g]
        send(at, at, up_send.at[k], up_recv.at[g], group_peer(k))
    pass_on(g, 0)
    for k in range(1, n_group):
        frm = lax.rem(g + k, n_group)
        arrive(gathered.at[place, frm], up_send.at[k], up_recv.at[frm], group_peer(k))
        pass_on(frm, k)
    for k in range(1, n_group):
        frm = lax.rem(g + k, n_group)
        at = diff.at[:, pl.ds(pl.multiple_of(frm * ROWS, ROWS), ROWS), :]
        arrive(at, diff_send.at[k], diff_recv.at[frm], group_peer(k))
    own_over = over[0]
    for dd in range(1, n_dp):
        own_over = jnp.where(d == dd, over[dd], own_over)
    for i in range(images):
        dmd_ref[i] = diff[i].astype(F32) * own_over[i : i + 1, 0:1]
    for turn in range(n_group):
        h = lax.rem(g + turn, n_group)
        for k in range(1, n_same):
            frm, device = same_core(k)
            at = gathered.at[frm, h]
            arrive(at, all_send.at[k, turn], all_recv.at[frm, h], device)
            send(at, at, core_send.at[k, turn], all_recv.at[frm, h], other_core)
    for turn in range(n_group):
        h = lax.rem(g + turn, n_group)
        for k in range(n_same):
            frm = same_core(k)[0] + n_dp - 2 * n_dp * lax.rem(s, 2)
            arrive(gathered.at[frm, h], core_send.at[k, turn], all_recv.at[frm, h], other_core)
    for o in range(n_plane):
        for h in range(n_group):
            at = (slice(h * ROWS, (h + 1) * ROWS), slice(o * chunk, (o + 1) * chunk))
            grad_ref[at] = gathered[o, h].astype(F32)
    for copy in sends:
        copy.wait_send()


def fits(shape, images, toks, channels, width, head):
    n_group, n_plane = shape["group"], shape["seq"] * shape["dp"]
    return (
        n_group == 4
        and channels == n_group * ROWS
        and images <= 8
        and toks % 128 == 0
        and head % 128 == 0
        and shape["seq"] % 2 == 0
        and width % (n_plane * 128) == 0
    )


def per_device(
    shape,
    noise_gen,
    noise_score,
    prev_latents,
    t_idx,
    w_in,
    w_qkv,
    w_out,
    w_final,
    mod_scale,
    mod_shift,
    saved_features,
):
    images, toks, channels = noise_gen.shape
    width, head = w_in.shape[2], w_out.shape[1]
    if not fits(shape, images, toks, channels, width, head):
        return per_device_plain(
            noise_gen,
            noise_score,
            prev_latents,
            t_idx,
            w_in,
            w_qkv,
            w_out,
            w_final,
            mod_scale,
            mod_shift,
            saved_features,
        )
    n_group, n_seq, n_dp = shape["group"], shape["seq"], shape["dp"]
    n_plane = n_seq * n_dp
    chunk = width // n_plane
    vmem = pl.BlockSpec(memory_space=pltpu.VMEM)
    hbm = pl.BlockSpec(memory_space=pltpu.HBM)
    dma = pltpu.SemaphoreType.DMA
    all_tokens = n_seq * toks
    total_in = n_group * n_plane
    prediction, dmd_grad, grad = pl.pallas_call(
        functools.partial(kernel, (n_group, n_seq, n_dp)),
        out_shape=(
            jax.ShapeDtypeStruct((images, channels, toks), F32),
            jax.ShapeDtypeStruct((images, channels, toks), F32),
            jax.ShapeDtypeStruct((channels, width), F32),
        ),
        in_specs=[hbm] * 11,
        out_specs=(vmem, vmem, vmem),
        scratch_shapes=[
            pltpu.VMEM((images, channels, toks), BF16),
            pltpu.VMEM((images, channels, toks), BF16),
            pltpu.VMEM((images, channels, toks), F32),
            pltpu.VMEM((channels, width), BF16),
            pltpu.VMEM((channels, head), BF16),
            pltpu.VMEM((1, width), F32),
            pltpu.VMEM((1, width), F32),
            pltpu.SMEM((images,), jnp.int32),
            pltpu.VMEM((width, 3 * head), BF16),
            pltpu.VMEM((channels, width), BF16),
            pltpu.VMEM((images, toks, width), BF16),
            pltpu.VMEM(((PARTS + 1) * channels + ROWS, width), BF16),
            pltpu.VMEM((n_seq, images, channels, toks), BF16),
            pltpu.VMEM((n_seq, 8, toks), F32),
            pltpu.VMEM((images, channels, toks), F32),
            pltpu.VMEM((images, all_tokens, head), BF16),
            pltpu.VMEM((images, n_seq, head, toks), BF16),
            pltpu.VMEM((images, head, all_tokens), BF16),
            pltpu.VMEM((n_seq, images, channels, toks), BF16),
            pltpu.VMEM((n_seq, images, channels, toks), BF16),
            pltpu.VMEM((n_group, images, ROWS, toks), BF16),
            pltpu.VMEM((n_group, images, ROWS, toks), BF16),
            pltpu.VMEM((images, channels, toks), BF16),
            pltpu.VMEM((total_in, 8, 128), F32),
            pltpu.VMEM((n_plane, images, ROWS, chunk), BF16),
            pltpu.VMEM((n_plane, images, ROWS, chunk), BF16),
            pltpu.VMEM((n_plane, n_group, ROWS, chunk), BF16),
            dma((13,)),
            dma((n_seq,)),
            dma((n_seq,)),
            dma((n_seq,)),
            dma((n_seq,)),
            dma((n_seq,)),
            dma((n_seq,)),
            dma((n_group,)),
            dma((n_group,)),
            dma((n_group,)),
            dma((n_group,)),
            dma((total_in,)),
            dma((total_in,)),
            dma((n_plane,)),
            dma((n_plane,)),
            dma((n_group,)),
            dma((n_group,)),
            dma((n_plane // 2, n_group)),
            dma((n_plane // 2, n_group)),
            dma((n_plane, n_group)),
        ],
        compiler_params=pltpu.CompilerParams(
            collective_id=0, has_side_effects=True, vmem_limit_bytes=48 * 1024 * 1024
        ),
    )(
        *(
            pltpu.with_memory_space_constraint(x, pltpu.HBM)
            for x in (
                t_idx,
                noise_gen.transpose(0, 2, 1),
                noise_score.transpose(0, 2, 1),
                prev_latents.transpose(0, 2, 1),
                w_in[0],
                w_qkv[0].transpose(1, 0, 2),
                w_out[0].T,
                w_final[0].T,
                mod_scale,
                mod_shift,
                saved_features,
            )
        ),
    )
    return prediction.transpose(0, 2, 1)[None], dmd_grad.transpose(0, 2, 1), grad.T


def solution(mesh):
    placed = (
        P("dp", "seq", None),
        P("dp", "seq", None),
        P("dp", "seq", None),
        P("dp"),
        P("group", None, None),
        P("group", None, None, "seq"),
        P("group", "seq", None),
        P("group", None, None),
        P("group", None),
        P("group", None),
        P("dp", "seq", None),
    )
    return jax.shard_map(
        functools.partial(per_device, dict(mesh.shape)),
        mesh=mesh,
        in_specs=placed,
        out_specs=(P("group", "dp", "seq", None), P("dp", "seq", None), P()),
        check_vma=False,
    )
```

```python
import functools
import math

import jax
import jax.numpy as jnp
from jax import lax
from jax.experimental import pallas as pl
from jax.experimental.pallas import tpu as pltpu
from jax.sharding import PartitionSpec as P

NTOK = 1024
NOISE_LEVEL_COUNT = 1000


def embed(latent, noise_level, w_in_here, scale, shift):
    projected = jnp.einsum("inp,pd->ind", latent, w_in_here, preferred_element_type=jnp.float32)
    normed = projected * lax.rsqrt(jnp.mean(projected * projected, axis=-1, keepdims=True) + 1e-06)
    return (normed * (1.0 + noise_level[:, None, None] * scale) + shift).astype(jnp.bfloat16)


def per_device_plain(
    noise_gen,
    noise_score,
    prev_latents,
    t_idx,
    w_in,
    w_qkv,
    w_out,
    w_final,
    mod_scale,
    mod_shift,
    saved_features,
):
    model_index = lax.axis_index("group")
    local_image_batch, rows_image, channels = noise_gen.shape
    width = w_in.shape[2]
    head_size = w_out.shape[1]
    level = (t_idx.astype(jnp.float32) + 0.5) / NOISE_LEVEL_COUNT
    noisy = (1.0 - level)[:, None, None] * prev_latents + level[:, None, None] * noise_score.astype(
        jnp.float32
    )
    is_generator = model_index == 0
    model_input = jnp.where(is_generator, noise_gen.astype(jnp.float32), noisy)
    noise_level = jnp.where(is_generator, jnp.ones_like(level), level)
    latent = model_input.astype(jnp.bfloat16)
    w_in_here = w_in[0]
    head_weight = w_qkv[0].reshape(width, 3 * head_size)
    scale = mod_scale[0]
    shift = mod_shift[0]
    features = embed(latent, noise_level, w_in_here, scale, shift)
    triple = jnp.einsum(
        "ind,de->ine",
        lax.all_gather(features, "seq", axis=1, tiled=True),
        head_weight,
        preferred_element_type=jnp.float32,
    ).astype(jnp.bfloat16)
    queries = triple[:, :, :head_size]
    keys = triple[:, :, head_size : 2 * head_size]
    value_rows = triple[:, :, 2 * head_size :]
    scores = jnp.einsum(
        "iqe,ike->iqk", queries, keys, preferred_element_type=jnp.float32
    ) / math.sqrt(head_size)
    probs = jax.nn.softmax(scores, axis=-1).astype(jnp.bfloat16)
    attention_result = jnp.einsum(
        "iqk,ike->iqe", probs, value_rows, preferred_element_type=jnp.float32
    ).astype(jnp.bfloat16)
    token_leading_layout = attention_result.transpose(1, 0, 2)
    output_layout = w_out[0]
    summed = (
        lax.psum_scatter(
            jnp.einsum(
                "sca,af->scf",
                token_leading_layout,
                output_layout,
                preferred_element_type=jnp.float32,
            ).astype(jnp.bfloat16),
            "seq",
            scatter_dimension=0,
            tiled=True,
        )
        .astype(jnp.float32)
        .transpose(1, 0, 2)
    )
    velocity = (
        jnp.einsum("ind,dp->inp", features, w_final[0], preferred_element_type=jnp.float32) + summed
    )
    prediction = model_input - noise_level[:, None, None] * velocity
    real_weight = jnp.where(model_index == 1, 2.5, jnp.where(model_index == 2, -1.5, 0.0))
    fake_weight = jnp.where(model_index == 3, 1.0, 0.0)
    real, fake = lax.psum((real_weight * prediction, fake_weight * prediction), "group")
    deviation = jnp.sum(jnp.abs(prev_latents - real), axis=(1, 2))
    total_dev = lax.psum(deviation, "seq")
    spread = total_dev / (NTOK * channels) + 1e-05
    dmd_grad = (fake - real) / spread[:, None, None]
    down = (-dmd_grad).astype(jnp.bfloat16)
    normalizer = 1.0 / math.sqrt(local_image_batch * lax.axis_size("dp") * NTOK)
    partial_grad = jnp.einsum(
        "ind,inp->dp", saved_features, down, preferred_element_type=jnp.float32
    )
    total_grad = lax.psum(partial_grad, ("seq", "dp"))
    return (prediction[None], dmd_grad, total_grad * normalizer)


F32 = jnp.float32
BF16 = jnp.bfloat16
MESH = pl.DeviceIdType.MESH
PARTS = 3
ROWS = 16


def dot(a, b):
    return jnp.dot(a, b, preferred_element_type=F32)


def dot_first(a, b):
    return lax.dot_general(a, b, (((0,), (0,)), ((), ())), preferred_element_type=F32)


def dot_last(a, b):
    return lax.dot_general(a, b, (((1,), (1,)), ((), ())), preferred_element_type=F32)


def split_parts(x):
    terms = []
    for _ in range(PARTS):
        term = x.astype(BF16)
        terms.append(term)
        x = x - term.astype(F32)
    return terms


def kernel(
    dims,
    t_hbm,
    noise_gen_hbm,
    noise_score_hbm,
    prev_hbm,
    w_in_hbm,
    w_qkv_hbm,
    w_out_hbm,
    w_final_hbm,
    scale_hbm,
    shift_hbm,
    saved_hbm,
    pred_ref,
    dmd_ref,
    grad_ref,
    noise_gen_ref,
    noise_score_ref,
    prev_ref,
    w_in_ref,
    w_out_ref,
    scale_ref,
    shift_ref,
    t_ref,
    w_qkv,
    w_final,
    saved,
    left,
    xg,
    rg,
    noisy,
    keys,
    queries,
    values,
    vel_out,
    vel_in,
    split_out,
    split_in,
    diff,
    dev,
    grad_out,
    grad_in,
    gathered,
    load_sem,
    x_send,
    x_recv,
    r_send,
    r_recv,
    vel_send,
    vel_recv,
    split_send,
    split_recv,
    diff_send,
    diff_recv,
    dev_send,
    dev_recv,
    grad_send,
    grad_recv,
    up_send,
    up_recv,
    all_send,
    core_send,
    all_recv,
):
    n_group, n_seq, n_dp = dims
    n_plane = n_seq * n_dp
    images, channels, toks = prev_ref.shape
    width = w_in_ref.shape[1]
    n_same = n_plane // 2
    head = w_out_ref.shape[1]
    chunk = grad_in.shape[3]
    g = lax.axis_index("group")
    s = lax.axis_index("seq")
    d = lax.axis_index("dp")
    place = s * n_dp + d
    here = g * n_plane + place

    pairs = [
        (noise_gen_hbm, noise_gen_ref),
        (noise_score_hbm, noise_score_ref),
        (prev_hbm, prev_ref),
        (w_in_hbm, w_in_ref),
        (scale_hbm, scale_ref),
        (shift_hbm, shift_ref),
        (w_final_hbm, w_final),
        (w_out_hbm, w_out_ref),
    ]
    pairs += [(w_qkv_hbm.at[c], w_qkv.at[:, c * head : (c + 1) * head]) for c in range(3)]
    pairs += [(saved_hbm, saved), (t_hbm, t_ref)]
    loads = [pltpu.make_async_copy(src, dst, load_sem.at[at]) for at, (src, dst) in enumerate(pairs)]
    for load in loads:
        load.start()

    barrier = pltpu.get_barrier_semaphore()
    others = [
        (dg, ds, dd)
        for dg in range(n_group)
        for ds in range(n_seq)
        for dd in range(n_dp)
        if dg or ds or dd
    ]

    def other(dg, ds, dd):
        gg, ss, dp = lax.rem(g + dg, n_group), lax.rem(s + ds, n_seq), lax.rem(d + dd, n_dp)
        return (gg * n_seq + ss) * n_dp + dp, {"group": gg, "seq": ss, "dp": dp}

    for shift in others:
        pl.semaphore_signal(barrier, inc=1, device_id=other(*shift)[1], device_id_type=MESH)

    generator = jnp.where(g == 0, 1.0, 0.0).astype(F32)

    def level(i, lanes):
        return (jnp.full((1, lanes), t_ref[i].astype(F32), F32) + 0.5) / NOISE_LEVEL_COUNT

    def own_level(i, lanes):
        return generator + (1.0 - generator) * level(i, lanes)

    for load in loads[:3] + loads[12:]:
        load.wait()
    for i in range(images):
        lv = level(i, toks)
        noisy[i] = (1.0 - lv) * prev_ref[i] + lv * noise_score_ref[i].astype(F32)
        model_input = generator * noise_gen_ref[i].astype(F32) + (1.0 - generator) * noisy[i]
        pred_ref[i] = model_input
        xg[0, i] = model_input.astype(BF16)

    pl.semaphore_wait(barrier, len(others))

    sends = []

    def send(src, dst, send_sem, recv_sem, device):
        copy = pltpu.make_async_remote_copy(
            src_ref=src,
            dst_ref=dst,
            send_sem=send_sem,
            recv_sem=recv_sem,
            device_id=device,
            device_id_type=MESH,
        )
        copy.start()
        sends.append(copy)

    def arrive(dst, send_sem, recv_sem, device):
        pltpu.make_async_remote_copy(
            src_ref=dst,
            dst_ref=dst,
            send_sem=send_sem,
            recv_sem=recv_sem,
            device_id=device,
            device_id_type=MESH,
        ).wait_recv()

    def seq_peer(k):
        return {"seq": lax.rem(s + k, n_seq)}

    for k in range(1, n_seq):
        send(xg.at[0], xg.at[k], x_send.at[k], x_recv.at[k], seq_peer(n_seq - k))

    for load in loads[3:6]:
        load.wait()
    both = jnp.concatenate([xg[0, i] for i in range(images)], axis=1)
    square = jnp.zeros((1, images * toks), F32)
    step = width // 4
    for at in range(0, width, step):
        projected = dot_first(w_in_ref[:, at : at + step], both)
        square = square + jnp.sum(projected * projected, axis=0, keepdims=True)
    inverse = lax.rsqrt(square * (1.0 / width) + 1e-06)
    rg[0] = jnp.concatenate(
        [inverse[:, i * toks : (i + 1) * toks] for i in range(images)]
        + [jnp.zeros((8 - images, toks), F32)],
        axis=0,
    )
    for k in range(1, n_seq):
        send(rg.at[0], rg.at[k], r_send.at[k], r_recv.at[k], seq_peer(n_seq - k))

    left[0:channels] = w_in_ref[...]
    scaled = split_parts(w_in_ref[...].astype(F32) * scale_ref[...])
    for at, term in enumerate(scaled):
        left[(at + 1) * channels : (at + 2) * channels] = term
    base = (PARTS + 1) * channels
    row = lax.broadcasted_iota(jnp.int32, (ROWS, width), 0)
    shift_rows = jnp.zeros((ROWS, width), F32)
    for at, term in enumerate(split_parts(shift_ref[...])):
        shift_rows = jnp.where(row == at, term.astype(F32), shift_rows)
    left[base : base + ROWS] = shift_rows.astype(BF16)

    for load in loads[6:11]:
        load.wait()
    maps = jnp.concatenate([dot(left[...], w_qkv[...]), dot_last(left[...], w_final[...])], axis=1)
    total = 3 * head + channels
    plain = maps[0:channels]
    per_level = sum(maps[(at + 1) * channels : (at + 2) * channels] for at in range(PARTS))
    bias_row = jnp.sum(maps[base : base + ROWS], axis=0, keepdims=True)
    row = lax.broadcasted_iota(jnp.int32, (ROWS, total), 0)
    bias_rows = jnp.zeros((ROWS, total), F32)
    for at, term in enumerate(split_parts(bias_row)):
        bias_rows = jnp.where(row == at, term.astype(F32), bias_rows)
    bias = dot_first(bias_rows.astype(BF16), jnp.ones((ROWS, toks), BF16))
    combined = [
        jnp.concatenate(split_parts((plain + own_level(i, total) * per_level).T), axis=1)
        for i in range(images)
    ]

    factor = math.log2(math.e) / math.sqrt(head)
    local = []
    for k in range(n_seq):
        if k:
            arrive(xg.at[k], x_send.at[k], x_recv.at[k], seq_peer(k))
            arrive(rg.at[k], r_send.at[k], r_recv.at[k], seq_peer(k))
        rows = total if k == 0 else 3 * head
        for i in range(images):
            x = xg[k, i]
            stacked = jnp.concatenate([x] * PARTS, axis=0)
            triple = dot(combined[i][:rows], stacked) * rg[k, i : i + 1, :] + bias[:rows]
            queries[i, k] = (triple[:head] * factor).astype(BF16)
            keys[i, k * toks : (k + 1) * toks] = triple[head : 2 * head].T.astype(BF16)
            values[i, :, k * toks : (k + 1) * toks] = triple[2 * head : 3 * head].astype(BF16)
            if k == 0:
                local.append(triple[3 * head :])

    own = []
    def group_peer(k):
        return {"group": lax.rem(g + k, n_group)}

    def part_rows(h):
        return pl.ds(pl.multiple_of(h * ROWS, ROWS), ROWS)

    for k in range(1, n_seq):
        split_in[g, k] = jnp.zeros((images, ROWS, toks), BF16)
    for k in list(range(1, n_seq)) + [0]:
        for i in range(images):
            scores = dot(keys[i], queries[i, k])
            weights = jnp.exp2(scores - jnp.max(scores, axis=0, keepdims=True))
            norm = 1.0 / jnp.sum(weights, axis=0, keepdims=True)
            attended = (dot(values[i], weights.astype(BF16)) * norm).astype(BF16)
            term = dot(w_out_ref[...], attended)
            if k == 0:
                term = term + local[i]
                own.append(term)
            vel_out[k, i] = term.astype(BF16)
        for dg in range(1, n_group):
            h = lax.rem(g + dg, n_group)
            send(
                vel_out.at[k, :, part_rows(h), :],
                split_in.at[g, k],
                split_send.at[dg, k],
                split_recv.at[g, k],
                {"group": h, "seq": lax.rem(s + k, n_seq)},
            )
        if k:
            send(vel_out.at[k], vel_in.at[k], vel_send.at[k], vel_recv.at[k], seq_peer(k))

    for k in range(1, n_seq):
        arrive(vel_in.at[k], vel_send.at[k], vel_recv.at[k], seq_peer(n_seq - k))
    for i in range(images):
        velocity = own[i]
        for k in range(1, n_seq):
            velocity = velocity + vel_in[k, i].astype(F32)
        pred_ref[i] = pred_ref[i] - own_level(i, toks) * velocity
        for h in range(n_group):
            split_out[h, i] = velocity[h * ROWS : (h + 1) * ROWS].astype(BF16)
    split_in[g, 0] = split_out[g]
    for dg in range(1, n_group):
        frm = lax.rem(g + dg, n_group)
        for k in range(n_seq):
            device = {"group": frm, "seq": lax.rem(s + n_seq - k, n_seq)}
            arrive(split_in.at[frm, k], split_send.at[dg, k], split_recv.at[frm, k], device)

    def model_velocity(h, i):
        return sum(split_in[h, k, i].astype(F32) for k in range(n_seq))

    part = part_rows(g)
    sums, mine = [], []
    for i in range(images):
        lv = level(i, toks)
        guided = 2.5 * model_velocity(1, i) - 1.5 * model_velocity(2, i)
        real = noisy[i, part, :] - lv * guided
        away = jnp.abs(prev_ref[i, part, :] - real)
        away = jnp.sum(jnp.sum(away, axis=0, keepdims=True), axis=1, keepdims=True)
        sums.append(jnp.broadcast_to(away, (1, 128)))
        mine.append((lv * (guided - model_velocity(3, i))).astype(BF16))
        diff[i, part, :] = mine[i]
    dev[here] = jnp.concatenate(sums + [jnp.zeros((8 - images, 128), F32)], axis=0)
    for at, shift in enumerate(others):
        send(dev.at[here], dev.at[here], dev_send.at[at], dev_recv.at[here], other(*shift)[1])
    loads[11].wait()
    for i in range(images):
        product = dot(mine[i], saved[i])
        for o in range(n_plane):
            grad_out[o, i] = product[:, o * chunk : (o + 1) * chunk].astype(BF16)

    def plane_peer(k):
        to = lax.rem(place + k, n_plane)
        return to, {"seq": to // n_dp, "dp": lax.rem(to, n_dp)}

    for k in range(1, n_plane):
        to, device = plane_peer(k)
        send(grad_out.at[to], grad_in.at[place], grad_send.at[k], grad_recv.at[place], device)
    grad_in[place] = grad_out[place]
    for k in range(1, n_group):
        at = diff.at[:, part, :]
        send(at, at, diff_send.at[k], diff_recv.at[g], group_peer(k))
    for at, shift in enumerate(others):
        there, device = other(*shift)
        arrive(dev.at[there], dev_send.at[at], dev_recv.at[there], device)
    over = []
    for dd in range(n_dp):
        away = dev[dd]
        for at in range(1, n_group * n_seq):
            away = away + dev[at * n_dp + dd]
        over.append(1.0 / (away * (1.0 / (n_seq * toks * channels)) + 1e-05))
    for k in range(1, n_plane):
        frm, device = plane_peer(k)
        arrive(grad_in.at[frm], grad_send.at[k], grad_recv.at[frm], device)
    normalizer = 1.0 / math.sqrt(images * n_dp * n_seq * toks)
    summed = jnp.zeros((ROWS, chunk), F32)
    for o in range(n_plane):
        for i in range(images):
            weight = over[o % n_dp][i : i + 1, 0:1] * -normalizer
            summed = summed + grad_in[o, i].astype(F32) * weight
    gathered[place, g] = summed.astype(BF16)
    other_core = {"seq": s + 1 - 2 * lax.rem(s, 2)}

    def same_core(k):
        seq, dp = lax.rem(s + 2 * (k // n_dp), n_seq), lax.rem(d + k % n_dp, n_dp)
        return seq * n_dp + dp, {"seq": seq, "dp": dp}

    def pass_on(h, turn):
        for k in range(1, n_same):
            at = gathered.at[place, h]
            send(at, at, all_send.at[k, turn], all_recv.at[place, h], same_core(k)[1])
        at = gathered.at[place, h]
        send(at, at, core_send.at[0, turn], all_recv.at[place, h], other_core)

    for k in range(1, n_group):
        at = gathered.at[place, g]
        send(at, at, up_send.at[k], up_recv.at[g], group_peer(k))
    pass_on(g, 0)
    for k in range(1, n_group):
        frm = lax.rem(g + k, n_group)
        arrive(gathered.at[place, frm], up_send.at[k], up_recv.at[frm], group_peer(k))
        pass_on(frm, k)
    for k in range(1, n_group):
        frm = lax.rem(g + k, n_group)
        at = diff.at[:, pl.ds(pl.multiple_of(frm * ROWS, ROWS), ROWS), :]
        arrive(at, diff_send.at[k], diff_recv.at[frm], group_peer(k))
    own_over = over[0]
    for dd in range(1, n_dp):
        own_over = jnp.where(d == dd, over[dd], own_over)
    for i in range(images):
        dmd_ref[i] = diff[i].astype(F32) * own_over[i : i + 1, 0:1]
    for turn in range(n_group):
        h = lax.rem(g + turn, n_group)
        for k in range(1, n_same):
            frm, device = same_core(k)
            at = gathered.at[frm, h]
            arrive(at, all_send.at[k, turn], all_recv.at[frm, h], device)
            send(at, at, core_send.at[k, turn], all_recv.at[frm, h], other_core)
    for turn in range(n_group):
        h = lax.rem(g + turn, n_group)
        for k in range(n_same):
            frm = same_core(k)[0] + n_dp - 2 * n_dp * lax.rem(s, 2)
            arrive(gathered.at[frm, h], core_send.at[k, turn], all_recv.at[frm, h], other_core)
    for o in range(n_plane):
        for h in range(n_group):
            at = (slice(h * ROWS, (h + 1) * ROWS), slice(o * chunk, (o + 1) * chunk))
            grad_ref[at] = gathered[o, h].astype(F32)
    for copy in sends:
        copy.wait_send()


def fits(shape, images, toks, channels, width, head):
    n_group, n_plane = shape["group"], shape["seq"] * shape["dp"]
    return (
        n_group == 4
        and channels == n_group * ROWS
        and images <= 8
        and toks % 128 == 0
        and head % 128 == 0
        and shape["seq"] % 2 == 0
        and width % (n_plane * 128) == 0
    )


def per_device(
    shape,
    noise_gen,
    noise_score,
    prev_latents,
    t_idx,
    w_in,
    w_qkv,
    w_out,
    w_final,
    mod_scale,
    mod_shift,
    saved_features,
):
    images, toks, channels = noise_gen.shape
    width, head = w_in.shape[2], w_out.shape[1]
    if not fits(shape, images, toks, channels, width, head):
        return per_device_plain(
            noise_gen,
            noise_score,
            prev_latents,
            t_idx,
            w_in,
            w_qkv,
            w_out,
            w_final,
            mod_scale,
            mod_shift,
            saved_features,
        )
    n_group, n_seq, n_dp = shape["group"], shape["seq"], shape["dp"]
    n_plane = n_seq * n_dp
    chunk = width // n_plane
    vmem = pl.BlockSpec(memory_space=pltpu.VMEM)
    hbm = pl.BlockSpec(memory_space=pltpu.HBM)
    dma = pltpu.SemaphoreType.DMA
    all_tokens = n_seq * toks
    total_in = n_group * n_plane
    prediction, dmd_grad, grad = pl.pallas_call(
        functools.partial(kernel, (n_group, n_seq, n_dp)),
        out_shape=(
            jax.ShapeDtypeStruct((images, channels, toks), F32),
            jax.ShapeDtypeStruct((images, channels, toks), F32),
            jax.ShapeDtypeStruct((channels, width), F32),
        ),
        in_specs=[hbm] * 11,
        out_specs=(vmem, vmem, vmem),
        scratch_shapes=[
            pltpu.VMEM((images, channels, toks), BF16),
            pltpu.VMEM((images, channels, toks), BF16),
            pltpu.VMEM((images, channels, toks), F32),
            pltpu.VMEM((channels, width), BF16),
            pltpu.VMEM((channels, head), BF16),
            pltpu.VMEM((1, width), F32),
            pltpu.VMEM((1, width), F32),
            pltpu.SMEM((images,), jnp.int32),
            pltpu.VMEM((width, 3 * head), BF16),
            pltpu.VMEM((channels, width), BF16),
            pltpu.VMEM((images, toks, width), BF16),
            pltpu.VMEM(((PARTS + 1) * channels + ROWS, width), BF16),
            pltpu.VMEM((n_seq, images, channels, toks), BF16),
            pltpu.VMEM((n_seq, 8, toks), F32),
            pltpu.VMEM((images, channels, toks), F32),
            pltpu.VMEM((images, all_tokens, head), BF16),
            pltpu.VMEM((images, n_seq, head, toks), BF16),
            pltpu.VMEM((images, head, all_tokens), BF16),
            pltpu.VMEM((n_seq, images, channels, toks), BF16),
            pltpu.VMEM((n_seq, images, channels, toks), BF16),
            pltpu.VMEM((n_group, images, ROWS, toks), BF16),
            pltpu.VMEM((n_group, n_seq, images, ROWS, toks), BF16),
            pltpu.VMEM((images, channels, toks), BF16),
            pltpu.VMEM((total_in, 8, 128), F32),
            pltpu.VMEM((n_plane, images, ROWS, chunk), BF16),
            pltpu.VMEM((n_plane, images, ROWS, chunk), BF16),
            pltpu.VMEM((n_plane, n_group, ROWS, chunk), BF16),
            dma((13,)),
            dma((n_seq,)),
            dma((n_seq,)),
            dma((n_seq,)),
            dma((n_seq,)),
            dma((n_seq,)),
            dma((n_seq,)),
            dma((n_group, n_seq)),
            dma((n_group, n_seq)),
            dma((n_group,)),
            dma((n_group,)),
            dma((total_in,)),
            dma((total_in,)),
            dma((n_plane,)),
            dma((n_plane,)),
            dma((n_group,)),
            dma((n_group,)),
            dma((n_plane // 2, n_group)),
            dma((n_plane // 2, n_group)),
            dma((n_plane, n_group)),
        ],
        compiler_params=pltpu.CompilerParams(
            collective_id=0, has_side_effects=True, vmem_limit_bytes=48 * 1024 * 1024
        ),
    )(
        *(
            pltpu.with_memory_space_constraint(x, pltpu.HBM)
            for x in (
                t_idx,
                noise_gen.transpose(0, 2, 1),
                noise_score.transpose(0, 2, 1),
                prev_latents.transpose(0, 2, 1),
                w_in[0],
                w_qkv[0].transpose(1, 0, 2),
                w_out[0].T,
                w_final[0].T,
                mod_scale,
                mod_shift,
                saved_features,
            )
        ),
    )
    return prediction.transpose(0, 2, 1)[None], dmd_grad.transpose(0, 2, 1), grad.T


def solution(mesh):
    placed = (
        P("dp", "seq", None),
        P("dp", "seq", None),
        P("dp", "seq", None),
        P("dp"),
        P("group", None, None),
        P("group", None, None, "seq"),
        P("group", "seq", None),
        P("group", None, None),
        P("group", None),
        P("group", None),
        P("dp", "seq", None),
    )
    return jax.shard_map(
        functools.partial(per_device, dict(mesh.shape)),
        mesh=mesh,
        in_specs=placed,
        out_specs=(P("group", "dp", "seq", None), P("dp", "seq", None), P()),
        check_vma=False,
    )
```

```python
import functools
import math

import jax
import jax.numpy as jnp
from jax import lax
from jax.experimental import pallas as pl
from jax.experimental.pallas import tpu as pltpu
from jax.sharding import PartitionSpec as P

NTOK = 1024
NOISE_LEVEL_COUNT = 1000


def embed(latent, noise_level, w_in_here, scale, shift):
    projected = jnp.einsum("inp,pd->ind", latent, w_in_here, preferred_element_type=jnp.float32)
    normed = projected * lax.rsqrt(jnp.mean(projected * projected, axis=-1, keepdims=True) + 1e-06)
    return (normed * (1.0 + noise_level[:, None, None] * scale) + shift).astype(jnp.bfloat16)


def per_device_plain(
    noise_gen,
    noise_score,
    prev_latents,
    t_idx,
    w_in,
    w_qkv,
    w_out,
    w_final,
    mod_scale,
    mod_shift,
    saved_features,
):
    model_index = lax.axis_index("group")
    local_image_batch, rows_image, channels = noise_gen.shape
    width = w_in.shape[2]
    head_size = w_out.shape[1]
    level = (t_idx.astype(jnp.float32) + 0.5) / NOISE_LEVEL_COUNT
    noisy = (1.0 - level)[:, None, None] * prev_latents + level[:, None, None] * noise_score.astype(
        jnp.float32
    )
    is_generator = model_index == 0
    model_input = jnp.where(is_generator, noise_gen.astype(jnp.float32), noisy)
    noise_level = jnp.where(is_generator, jnp.ones_like(level), level)
    latent = model_input.astype(jnp.bfloat16)
    w_in_here = w_in[0]
    head_weight = w_qkv[0].reshape(width, 3 * head_size)
    scale = mod_scale[0]
    shift = mod_shift[0]
    features = embed(latent, noise_level, w_in_here, scale, shift)
    triple = jnp.einsum(
        "ind,de->ine",
        lax.all_gather(features, "seq", axis=1, tiled=True),
        head_weight,
        preferred_element_type=jnp.float32,
    ).astype(jnp.bfloat16)
    queries = triple[:, :, :head_size]
    keys = triple[:, :, head_size : 2 * head_size]
    value_rows = triple[:, :, 2 * head_size :]
    scores = jnp.einsum(
        "iqe,ike->iqk", queries, keys, preferred_element_type=jnp.float32
    ) / math.sqrt(head_size)
    probs = jax.nn.softmax(scores, axis=-1).astype(jnp.bfloat16)
    attention_result = jnp.einsum(
        "iqk,ike->iqe", probs, value_rows, preferred_element_type=jnp.float32
    ).astype(jnp.bfloat16)
    token_leading_layout = attention_result.transpose(1, 0, 2)
    output_layout = w_out[0]
    summed = (
        lax.psum_scatter(
            jnp.einsum(
                "sca,af->scf",
                token_leading_layout,
                output_layout,
                preferred_element_type=jnp.float32,
            ).astype(jnp.bfloat16),
            "seq",
            scatter_dimension=0,
            tiled=True,
        )
        .astype(jnp.float32)
        .transpose(1, 0, 2)
    )
    velocity = (
        jnp.einsum("ind,dp->inp", features, w_final[0], preferred_element_type=jnp.float32) + summed
    )
    prediction = model_input - noise_level[:, None, None] * velocity
    real_weight = jnp.where(model_index == 1, 2.5, jnp.where(model_index == 2, -1.5, 0.0))
    fake_weight = jnp.where(model_index == 3, 1.0, 0.0)
    real, fake = lax.psum((real_weight * prediction, fake_weight * prediction), "group")
    deviation = jnp.sum(jnp.abs(prev_latents - real), axis=(1, 2))
    total_dev = lax.psum(deviation, "seq")
    spread = total_dev / (NTOK * channels) + 1e-05
    dmd_grad = (fake - real) / spread[:, None, None]
    down = (-dmd_grad).astype(jnp.bfloat16)
    normalizer = 1.0 / math.sqrt(local_image_batch * lax.axis_size("dp") * NTOK)
    partial_grad = jnp.einsum(
        "ind,inp->dp", saved_features, down, preferred_element_type=jnp.float32
    )
    total_grad = lax.psum(partial_grad, ("seq", "dp"))
    return (prediction[None], dmd_grad, total_grad * normalizer)


F32 = jnp.float32
BF16 = jnp.bfloat16
MESH = pl.DeviceIdType.MESH
PARTS = 3
ROWS = 16


def dot(a, b):
    return jnp.dot(a, b, preferred_element_type=F32)


def dot_first(a, b):
    return lax.dot_general(a, b, (((0,), (0,)), ((), ())), preferred_element_type=F32)


def dot_last(a, b):
    return lax.dot_general(a, b, (((1,), (1,)), ((), ())), preferred_element_type=F32)


def split_parts(x):
    terms = []
    for _ in range(PARTS):
        term = x.astype(BF16)
        terms.append(term)
        x = x - term.astype(F32)
    return terms


def kernel(
    dims,
    t_hbm,
    noise_gen_hbm,
    noise_score_hbm,
    prev_hbm,
    w_in_hbm,
    w_qkv_hbm,
    w_out_hbm,
    w_final_hbm,
    scale_hbm,
    shift_hbm,
    saved_hbm,
    pred_ref,
    dmd_ref,
    grad_ref,
    noise_gen_ref,
    noise_score_ref,
    prev_ref,
    w_in_ref,
    w_out_ref,
    scale_ref,
    shift_ref,
    t_ref,
    w_qkv,
    w_final,
    saved,
    left,
    xg,
    rg,
    noisy,
    keys,
    queries,
    values,
    vel_out,
    vel_in,
    split_out,
    split_in,
    diff,
    dev,
    grad_out,
    grad_in,
    gathered,
    load_sem,
    x_send,
    x_recv,
    r_send,
    r_recv,
    vel_send,
    vel_recv,
    split_send,
    split_recv,
    diff_send,
    diff_recv,
    dev_send,
    dev_recv,
    grad_send,
    grad_recv,
    up_send,
    up_recv,
    all_send,
    core_send,
    all_recv,
):
    n_group, n_seq, n_dp = dims
    n_plane = n_seq * n_dp
    images, channels, toks = prev_ref.shape
    width = w_in_ref.shape[1]
    n_same = n_plane // 2
    head = w_out_ref.shape[1]
    chunk = grad_in.shape[3]
    g = lax.axis_index("group")
    s = lax.axis_index("seq")
    d = lax.axis_index("dp")
    place = s * n_dp + d
    here = g * n_plane + place

    pairs = [
        (noise_gen_hbm, noise_gen_ref),
        (noise_score_hbm, noise_score_ref),
        (prev_hbm, prev_ref),
        (w_in_hbm, w_in_ref),
        (scale_hbm, scale_ref),
        (shift_hbm, shift_ref),
        (w_final_hbm, w_final),
        (w_out_hbm, w_out_ref),
    ]
    pairs += [(w_qkv_hbm.at[c], w_qkv.at[:, c * head : (c + 1) * head]) for c in range(3)]
    pairs += [(saved_hbm, saved), (t_hbm, t_ref)]
    loads = [pltpu.make_async_copy(src, dst, load_sem.at[at]) for at, (src, dst) in enumerate(pairs)]
    for load in loads:
        load.start()

    barrier = pltpu.get_barrier_semaphore()
    others = [
        (dg, ds, dd)
        for dg in range(n_group)
        for ds in range(n_seq)
        for dd in range(n_dp)
        if dg or ds or dd
    ]

    def other(dg, ds, dd):
        gg, ss, dp = lax.rem(g + dg, n_group), lax.rem(s + ds, n_seq), lax.rem(d + dd, n_dp)
        return (gg * n_seq + ss) * n_dp + dp, {"group": gg, "seq": ss, "dp": dp}

    for shift in others:
        pl.semaphore_signal(barrier, inc=1, device_id=other(*shift)[1], device_id_type=MESH)

    generator = jnp.where(g == 0, 1.0, 0.0).astype(F32)

    def level(i, lanes):
        return (jnp.full((1, lanes), t_ref[i].astype(F32), F32) + 0.5) / NOISE_LEVEL_COUNT

    def own_level(i, lanes):
        return generator + (1.0 - generator) * level(i, lanes)

    for load in loads[:3] + loads[12:]:
        load.wait()
    for i in range(images):
        lv = level(i, toks)
        noisy[i] = (1.0 - lv) * prev_ref[i] + lv * noise_score_ref[i].astype(F32)
        model_input = generator * noise_gen_ref[i].astype(F32) + (1.0 - generator) * noisy[i]
        pred_ref[i] = model_input
        xg[0, i] = model_input.astype(BF16)

    for load in loads[3:6]:
        load.wait()
    both = jnp.concatenate([xg[0, i] for i in range(images)], axis=1)
    square = jnp.zeros((1, images * toks), F32)
    step = width // 4
    for at in range(0, width, step):
        projected = dot_first(w_in_ref[:, at : at + step], both)
        square = square + jnp.sum(projected * projected, axis=0, keepdims=True)
    inverse = lax.rsqrt(square * (1.0 / width) + 1e-06)
    rg[0] = jnp.concatenate(
        [inverse[:, i * toks : (i + 1) * toks] for i in range(images)]
        + [jnp.zeros((8 - images, toks), F32)],
        axis=0,
    )
    pl.semaphore_wait(barrier, len(others))

    sends = []

    def send(src, dst, send_sem, recv_sem, device):
        copy = pltpu.make_async_remote_copy(
            src_ref=src,
            dst_ref=dst,
            send_sem=send_sem,
            recv_sem=recv_sem,
            device_id=device,
            device_id_type=MESH,
        )
        copy.start()
        sends.append(copy)

    def arrive(dst, send_sem, recv_sem, device):
        pltpu.make_async_remote_copy(
            src_ref=dst,
            dst_ref=dst,
            send_sem=send_sem,
            recv_sem=recv_sem,
            device_id=device,
            device_id_type=MESH,
        ).wait_recv()

    def seq_peer(k):
        return {"seq": lax.rem(s + k, n_seq)}

    for k in range(1, n_seq):
        send(xg.at[0], xg.at[k], x_send.at[k], x_recv.at[k], seq_peer(n_seq - k))

    for k in range(1, n_seq):
        send(rg.at[0], rg.at[k], r_send.at[k], r_recv.at[k], seq_peer(n_seq - k))

    left[0:channels] = w_in_ref[...]
    scaled = split_parts(w_in_ref[...].astype(F32) * scale_ref[...])
    for at, term in enumerate(scaled):
        left[(at + 1) * channels : (at + 2) * channels] = term
    base = (PARTS + 1) * channels
    row = lax.broadcasted_iota(jnp.int32, (ROWS, width), 0)
    shift_rows = jnp.zeros((ROWS, width), F32)
    for at, term in enumerate(split_parts(shift_ref[...])):
        shift_rows = jnp.where(row == at, term.astype(F32), shift_rows)
    left[base : base + ROWS] = shift_rows.astype(BF16)

    for load in loads[6:11]:
        load.wait()
    maps = jnp.concatenate([dot(left[...], w_qkv[...]), dot_last(left[...], w_final[...])], axis=1)
    total = 3 * head + channels
    plain = maps[0:channels]
    per_level = sum(maps[(at + 1) * channels : (at + 2) * channels] for at in range(PARTS))
    bias_row = jnp.sum(maps[base : base + ROWS], axis=0, keepdims=True)
    row = lax.broadcasted_iota(jnp.int32, (ROWS, total), 0)
    bias_rows = jnp.zeros((ROWS, total), F32)
    for at, term in enumerate(split_parts(bias_row)):
        bias_rows = jnp.where(row == at, term.astype(F32), bias_rows)
    bias = dot_first(bias_rows.astype(BF16), jnp.ones((ROWS, toks), BF16))
    combined = [
        jnp.concatenate(split_parts((plain + own_level(i, total) * per_level).T), axis=1)
        for i in range(images)
    ]

    factor = math.log2(math.e) / math.sqrt(head)
    local = []
    for k in range(n_seq):
        if k:
            arrive(xg.at[k], x_send.at[k], x_recv.at[k], seq_peer(k))
            arrive(rg.at[k], r_send.at[k], r_recv.at[k], seq_peer(k))
        rows = total if k == 0 else 3 * head
        for i in range(images):
            x = xg[k, i]
            stacked = jnp.concatenate([x] * PARTS, axis=0)
            triple = dot(combined[i][:rows], stacked) * rg[k, i : i + 1, :] + bias[:rows]
            queries[i, k] = (triple[:head] * factor).astype(BF16)
            keys[i, k * toks : (k + 1) * toks] = triple[head : 2 * head].T.astype(BF16)
            values[i, :, k * toks : (k + 1) * toks] = triple[2 * head : 3 * head].astype(BF16)
            if k == 0:
                local.append(triple[3 * head :])

    own = []
    def group_peer(k):
        return {"group": lax.rem(g + k, n_group)}

    def part_rows(h):
        return pl.ds(pl.multiple_of(h * ROWS, ROWS), ROWS)

    for k in range(1, n_seq):
        split_in[g, k] = jnp.zeros((images, ROWS, toks), BF16)
    for k in list(range(1, n_seq)) + [0]:
        for i in range(images):
            scores = dot(keys[i], queries[i, k])
            weights = jnp.exp2(scores - jnp.max(scores, axis=0, keepdims=True))
            norm = 1.0 / jnp.sum(weights, axis=0, keepdims=True)
            attended = (dot(values[i], weights.astype(BF16)) * norm).astype(BF16)
            term = dot(w_out_ref[...], attended)
            if k == 0:
                term = term + local[i]
                own.append(term)
            vel_out[k, i] = term.astype(BF16)
        for dg in range(1, n_group):
            h = lax.rem(g + dg, n_group)
            send(
                vel_out.at[k, :, part_rows(h), :],
                split_in.at[g, k],
                split_send.at[dg, k],
                split_recv.at[g, k],
                {"group": h, "seq": lax.rem(s + k, n_seq)},
            )
        if k:
            send(vel_out.at[k], vel_in.at[k], vel_send.at[k], vel_recv.at[k], seq_peer(k))

    for k in range(1, n_seq):
        arrive(vel_in.at[k], vel_send.at[k], vel_recv.at[k], seq_peer(n_seq - k))
    for i in range(images):
        velocity = own[i]
        for k in range(1, n_seq):
            velocity = velocity + vel_in[k, i].astype(F32)
        pred_ref[i] = pred_ref[i] - own_level(i, toks) * velocity
        for h in range(n_group):
            split_out[h, i] = velocity[h * ROWS : (h + 1) * ROWS].astype(BF16)
    split_in[g, 0] = split_out[g]
    for dg in range(1, n_group):
        frm = lax.rem(g + dg, n_group)
        for k in range(n_seq):
            device = {"group": frm, "seq": lax.rem(s + n_seq - k, n_seq)}
            arrive(split_in.at[frm, k], split_send.at[dg, k], split_recv.at[frm, k], device)

    def model_velocity(h, i):
        return sum(split_in[h, k, i].astype(F32) for k in range(n_seq))

    part = part_rows(g)
    sums, mine = [], []
    for i in range(images):
        lv = level(i, toks)
        guided = 2.5 * model_velocity(1, i) - 1.5 * model_velocity(2, i)
        real = noisy[i, part, :] - lv * guided
        away = jnp.abs(prev_ref[i, part, :] - real)
        away = jnp.sum(jnp.sum(away, axis=0, keepdims=True), axis=1, keepdims=True)
        sums.append(jnp.broadcast_to(away, (1, 128)))
        mine.append((lv * (guided - model_velocity(3, i))).astype(BF16))
        diff[i, part, :] = mine[i]
    dev[here] = jnp.concatenate(sums + [jnp.zeros((8 - images, 128), F32)], axis=0)
    for at, shift in enumerate(others):
        send(dev.at[here], dev.at[here], dev_send.at[at], dev_recv.at[here], other(*shift)[1])
    loads[11].wait()
    for i in range(images):
        product = dot(mine[i], saved[i])
        for o in range(n_plane):
            grad_out[o, i] = product[:, o * chunk : (o + 1) * chunk].astype(BF16)

    def plane_peer(k):
        to = lax.rem(place + k, n_plane)
        return to, {"seq": to // n_dp, "dp": lax.rem(to, n_dp)}

    for k in range(1, n_plane):
        to, device = plane_peer(k)
        send(grad_out.at[to], grad_in.at[place], grad_send.at[k], grad_recv.at[place], device)
    grad_in[place] = grad_out[place]
    for k in range(1, n_group):
        at = diff.at[:, part, :]
        send(at, at, diff_send.at[k], diff_recv.at[g], group_peer(k))
    for at, shift in enumerate(others):
        there, device = other(*shift)
        arrive(dev.at[there], dev_send.at[at], dev_recv.at[there], device)
    over = []
    for dd in range(n_dp):
        away = dev[dd]
        for at in range(1, n_group * n_seq):
            away = away + dev[at * n_dp + dd]
        over.append(1.0 / (away * (1.0 / (n_seq * toks * channels)) + 1e-05))
    for k in range(1, n_plane):
        frm, device = plane_peer(k)
        arrive(grad_in.at[frm], grad_send.at[k], grad_recv.at[frm], device)
    normalizer = 1.0 / math.sqrt(images * n_dp * n_seq * toks)
    summed = jnp.zeros((ROWS, chunk), F32)
    for o in range(n_plane):
        for i in range(images):
            weight = over[o % n_dp][i : i + 1, 0:1] * -normalizer
            summed = summed + grad_in[o, i].astype(F32) * weight
    gathered[place, g] = summed.astype(BF16)
    other_core = {"seq": s + 1 - 2 * lax.rem(s, 2)}

    def same_core(k):
        seq, dp = lax.rem(s + 2 * (k // n_dp), n_seq), lax.rem(d + k % n_dp, n_dp)
        return seq * n_dp + dp, {"seq": seq, "dp": dp}

    def pass_on(h, turn):
        for k in range(1, n_same):
            at = gathered.at[place, h]
            send(at, at, all_send.at[k, turn], all_recv.at[place, h], same_core(k)[1])
        at = gathered.at[place, h]
        send(at, at, core_send.at[0, turn], all_recv.at[place, h], other_core)

    for k in range(1, n_group):
        at = gathered.at[place, g]
        send(at, at, up_send.at[k], up_recv.at[g], group_peer(k))
    pass_on(g, 0)
    for k in range(1, n_group):
        frm = lax.rem(g + k, n_group)
        arrive(gathered.at[place, frm], up_send.at[k], up_recv.at[frm], group_peer(k))
        pass_on(frm, k)
    for k in range(1, n_group):
        frm = lax.rem(g + k, n_group)
        at = diff.at[:, pl.ds(pl.multiple_of(frm * ROWS, ROWS), ROWS), :]
        arrive(at, diff_send.at[k], diff_recv.at[frm], group_peer(k))
    own_over = over[0]
    for dd in range(1, n_dp):
        own_over = jnp.where(d == dd, over[dd], own_over)
    for i in range(images):
        dmd_ref[i] = diff[i].astype(F32) * own_over[i : i + 1, 0:1]
    for turn in range(n_group):
        h = lax.rem(g + turn, n_group)
        for k in range(1, n_same):
            frm, device = same_core(k)
            at = gathered.at[frm, h]
            arrive(at, all_send.at[k, turn], all_recv.at[frm, h], device)
            send(at, at, core_send.at[k, turn], all_recv.at[frm, h], other_core)
    for turn in range(n_group):
        h = lax.rem(g + turn, n_group)
        for k in range(n_same):
            frm = same_core(k)[0] + n_dp - 2 * n_dp * lax.rem(s, 2)
            arrive(gathered.at[frm, h], core_send.at[k, turn], all_recv.at[frm, h], other_core)
    for o in range(n_plane):
        for h in range(n_group):
            at = (slice(h * ROWS, (h + 1) * ROWS), slice(o * chunk, (o + 1) * chunk))
            grad_ref[at] = gathered[o, h].astype(F32)
    for copy in sends:
        copy.wait_send()


def fits(shape, images, toks, channels, width, head):
    n_group, n_plane = shape["group"], shape["seq"] * shape["dp"]
    return (
        n_group == 4
        and channels == n_group * ROWS
        and images <= 8
        and toks % 128 == 0
        and head % 128 == 0
        and shape["seq"] % 2 == 0
        and width % (n_plane * 128) == 0
    )


def per_device(
    shape,
    noise_gen,
    noise_score,
    prev_latents,
    t_idx,
    w_in,
    w_qkv,
    w_out,
    w_final,
    mod_scale,
    mod_shift,
    saved_features,
):
    images, toks, channels = noise_gen.shape
    width, head = w_in.shape[2], w_out.shape[1]
    if not fits(shape, images, toks, channels, width, head):
        return per_device_plain(
            noise_gen,
            noise_score,
            prev_latents,
            t_idx,
            w_in,
            w_qkv,
            w_out,
            w_final,
            mod_scale,
            mod_shift,
            saved_features,
        )
    n_group, n_seq, n_dp = shape["group"], shape["seq"], shape["dp"]
    n_plane = n_seq * n_dp
    chunk = width // n_plane
    vmem = pl.BlockSpec(memory_space=pltpu.VMEM)
    hbm = pl.BlockSpec(memory_space=pltpu.HBM)
    dma = pltpu.SemaphoreType.DMA
    all_tokens = n_seq * toks
    total_in = n_group * n_plane
    prediction, dmd_grad, grad = pl.pallas_call(
        functools.partial(kernel, (n_group, n_seq, n_dp)),
        out_shape=(
            jax.ShapeDtypeStruct((images, channels, toks), F32),
            jax.ShapeDtypeStruct((images, channels, toks), F32),
            jax.ShapeDtypeStruct((channels, width), F32),
        ),
        in_specs=[hbm] * 11,
        out_specs=(vmem, vmem, vmem),
        scratch_shapes=[
            pltpu.VMEM((images, channels, toks), BF16),
            pltpu.VMEM((images, channels, toks), BF16),
            pltpu.VMEM((images, channels, toks), F32),
            pltpu.VMEM((channels, width), BF16),
            pltpu.VMEM((channels, head), BF16),
            pltpu.VMEM((1, width), F32),
            pltpu.VMEM((1, width), F32),
            pltpu.SMEM((images,), jnp.int32),
            pltpu.VMEM((width, 3 * head), BF16),
            pltpu.VMEM((channels, width), BF16),
            pltpu.VMEM((images, toks, width), BF16),
            pltpu.VMEM(((PARTS + 1) * channels + ROWS, width), BF16),
            pltpu.VMEM((n_seq, images, channels, toks), BF16),
            pltpu.VMEM((n_seq, 8, toks), F32),
            pltpu.VMEM((images, channels, toks), F32),
            pltpu.VMEM((images, all_tokens, head), BF16),
            pltpu.VMEM((images, n_seq, head, toks), BF16),
            pltpu.VMEM((images, head, all_tokens), BF16),
            pltpu.VMEM((n_seq, images, channels, toks), BF16),
            pltpu.VMEM((n_seq, images, channels, toks), BF16),
            pltpu.VMEM((n_group, images, ROWS, toks), BF16),
            pltpu.VMEM((n_group, n_seq, images, ROWS, toks), BF16),
            pltpu.VMEM((images, channels, toks), BF16),
            pltpu.VMEM((total_in, 8, 128), F32),
            pltpu.VMEM((n_plane, images, ROWS, chunk), BF16),
            pltpu.VMEM((n_plane, images, ROWS, chunk), BF16),
            pltpu.VMEM((n_plane, n_group, ROWS, chunk), BF16),
            dma((13,)),
            dma((n_seq,)),
            dma((n_seq,)),
            dma((n_seq,)),
            dma((n_seq,)),
            dma((n_seq,)),
            dma((n_seq,)),
            dma((n_group, n_seq)),
            dma((n_group, n_seq)),
            dma((n_group,)),
            dma((n_group,)),
            dma((total_in,)),
            dma((total_in,)),
            dma((n_plane,)),
            dma((n_plane,)),
            dma((n_group,)),
            dma((n_group,)),
            dma((n_plane // 2, n_group)),
            dma((n_plane // 2, n_group)),
            dma((n_plane, n_group)),
        ],
        compiler_params=pltpu.CompilerParams(
            collective_id=0, has_side_effects=True, vmem_limit_bytes=48 * 1024 * 1024
        ),
    )(
        *(
            pltpu.with_memory_space_constraint(x, pltpu.HBM)
            for x in (
                t_idx,
                noise_gen.transpose(0, 2, 1),
                noise_score.transpose(0, 2, 1),
                prev_latents.transpose(0, 2, 1),
                w_in[0],
                w_qkv[0].transpose(1, 0, 2),
                w_out[0].T,
                w_final[0].T,
                mod_scale,
                mod_shift,
                saved_features,
            )
        ),
    )
    return prediction.transpose(0, 2, 1)[None], dmd_grad.transpose(0, 2, 1), grad.T


def solution(mesh):
    placed = (
        P("dp", "seq", None),
        P("dp", "seq", None),
        P("dp", "seq", None),
        P("dp"),
        P("group", None, None),
        P("group", None, None, "seq"),
        P("group", "seq", None),
        P("group", None, None),
        P("group", None),
        P("group", None),
        P("dp", "seq", None),
    )
    return jax.shard_map(
        functools.partial(per_device, dict(mesh.shape)),
        mesh=mesh,
        in_specs=placed,
        out_specs=(P("group", "dp", "seq", None), P("dp", "seq", None), P()),
        check_vma=False,
    )
```
